128 devices in a mesh: row: 16 (over x, y_hi, core), col: 8 (over y_lo, z).
Axes of the slice: x: 4, y: 4 (y_hi: 2, y_lo: 2; y = y_hi * 2 + y_lo), z: 4, core: 2. Of those that a mesh axis runs over, the one named last changes fastest.
Arguments:
- iterate: bfloat16 [4096, 12288], P('row', 'col'), may hold values from -0.0546875 to 0.0546875
Outputs:
- update: bfloat16 [4096, 12288], P('row', 'col')
The draws below stay inside these ranges and needn't reach their ends.
All inputs are finite; a program needn't handle non-finite values.
Results may differ from the reference program's by a relative error of at most 0.03.
Values may be sent and summed in bfloat16 or wider, within the bound.
No kernel may reach another device: no remote copies, remote signals or barrier semaphores. Data moves between devices by JAX's collectives and lax.ppermute only.
A program may use at most 64 MiB of HBM per device.

```python
import math
import jax
import jax.numpy as jnp

MATRIX_ROWS = 4096
MATRIX_COLS = 12288


def level_of(rng, extent, pieces, smallest, top_value):
    loudness, own = 1.0, jax.random.fold_in(rng, 6)
    for position, parts in pieces:
        draws = jnp.exp(jax.random.uniform(jax.random.fold_in(own, position), (parts,), jnp.float32, smallest / len(pieces), top_value / len(pieces)))
        loudness = loudness * jnp.repeat(draws, extent[position] // parts).reshape([-1 if axis == position else 1 for axis in range(len(extent))])
    return loudness


def gaussian(own_key, shape, deviation, bound, shards=(), dtype=jnp.bfloat16):
    result = jax.random.normal(own_key, shape, jnp.float32) * deviation
    if len(shards) > 0:
        result = level_of(own_key, shape, shards, -0.22, 0.18) * result
    return jnp.clip(result, min=-bound, max=bound).astype(dtype)


def setup_inputs(seed: int = 0) -> dict:
    arg_keys = jax.random.split(jax.random.key(seed), 2)
    return {
        "iterate": gaussian(arg_keys[0], (MATRIX_ROWS, MATRIX_COLS), MATRIX_COLS ** -0.5, 0.0546875, ((0, 16), (1, 8))),
    }


linear_coef = 3.4445
cubic_coef = -4.775
quintic_coef = 2.0315

def reference(iterate):
    gram = jnp.dot(iterate, iterate.T, preferred_element_type=jnp.float32).astype(jnp.bfloat16)
    square = jnp.dot(gram, gram, preferred_element_type=jnp.float32)
    mixing = (cubic_coef * gram.astype(jnp.float32) + quintic_coef * square).astype(jnp.bfloat16)
    applied = jnp.dot(mixing, iterate, preferred_element_type=jnp.float32)
    update = linear_coef * iterate.astype(jnp.float32) + applied
    return (math.sqrt(MATRIX_COLS) * update).astype(jnp.bfloat16)
```

```python
import functools
import math

import jax
import jax.numpy as jnp
from jax import lax
from jax.experimental import pallas as pl
from jax.experimental.pallas import tpu as pltpu
from jax.sharding import PartitionSpec as P

linear_coef = 3.4445
cubic_coef = -4.775
quintic_coef = 2.0315

NX, NY, NC, NZ = 4, 2, 2, 4
BLOCK = 256
TILE = 2 * BLOCK
SLOTS = [(0, 0), (0, 1), (0, 3), (0, 2), (1, 0), (1, 1), (1, 3), (1, 2)]
MIB = 1 << 20


def pairs(move):
    out = []
    for x in range(NX):
        for yh in range(NY):
            for core in range(NC):
                for yl in range(NY):
                    for z in range(NZ):
                        source = ((x * 2 + yh) * 2 + core) * 8 + yl * 4 + z
                        a, b, c, d, e = move(x, yh, core, yl, z)
                        a, e = a % NX, e % NZ
                        out.append((source, ((a * 2 + b) * 2 + c) * 8 + d * 4 + e))
    return out


def way(core):
    return 1 - 2 * core


MOVES = {
    "core": lambda x, yh, c, yl, z: (x, yh, 1 - c, yl, z),
    "yh": lambda x, yh, c, yl, z: (x, 1 - yh, c, yl, z),
    "yl": lambda x, yh, c, yl, z: (x, yh, c, 1 - yl, z),
    "x_fore": lambda x, yh, c, yl, z: (x + way(c), yh, c, yl, z),
    "x_back": lambda x, yh, c, yl, z: (x - way(c), yh, c, yl, z),
    "z_fore": lambda x, yh, c, yl, z: (x, yh, c, yl, z + way(c)),
    "z_back": lambda x, yh, c, yl, z: (x, yh, c, yl, z - way(c)),
}
for _dy, _dz in SLOTS[1:]:
    MOVES[(_dy, _dz)] = lambda x, yh, c, yl, z, _dy=_dy, _dz=_dz: (x, yh, c, (yl + _dy) % 2, z + _dz)


def send(value, move):
    return lax.ppermute(value, ("row", "col"), pairs(MOVES[move]))


def place(delta, core):
    delta = lax.rem(delta + 8, 4)
    side = jnp.where(delta == 3 - 2 * core, 1, 2)
    return jnp.where(delta == 0, 0, jnp.where(delta == 2, 3, side))


def ahead(position, core):
    return (0, 2 * core - 1, 1 - 2 * core, 2)[position]


def nt(left, right):
    return lax.dot_general(left, right, (((1,), (1,)), ((), ())), preferred_element_type=jnp.float32)


def nn(left, right):
    return lax.dot_general(left, right, (((1,), (0,)), ((), ())), preferred_element_type=jnp.float32)


def gram_near_kernel(own, other, fore, fore_other, back, back_other, across, out, acc):
    step = pl.program_id(0)

    @pl.when(step == 0)
    def _():
        acc[...] = jnp.zeros_like(acc)

    for r, rows in enumerate((own, across)):
        for q, cols in enumerate((own, other, fore, fore_other, back, back_other)):
            acc[r, q // 2, :, (q % 2) * BLOCK : (q % 2 + 1) * BLOCK] += nt(rows[...], cols[...])

    @pl.when(step == pl.num_programs(0) - 1)
    def _():
        out[...] = acc[...].astype(out.dtype)


def gram_far_kernel(where, own, across, far, far_other, near, *rest):
    outs, (acc, tiles) = rest[:8], rest[8:]
    step = pl.program_id(0)

    @pl.when(step == 0)
    def _():
        acc[...] = jnp.zeros_like(acc)

    for r, rows in enumerate((own, across)):
        for q, cols in enumerate((far, far_other)):
            acc[r, :, q * BLOCK : (q + 1) * BLOCK] += nt(rows[...], cols[...])

    @pl.when(step == pl.num_programs(0) - 1)
    def _():
        x, yh, core, yl, z = (where[i] for i in range(5))
        for r in range(2):
            tiles[r, 0:3] = near[r]
            tiles[r, 3] = acc[r].astype(tiles.dtype)
        for out, (dy, dz) in zip(outs, SLOTS):
            row = lax.rem(yl + dy + yh, 2)
            out[...] = tiles[row, place(z + dz - x, core)]


def square_kernel(where, *rest):
    left, right, (mine, theirs), (held,) = rest[:8], rest[8:16], rest[16:18], rest[18:]
    x, yh, core, yl, z = (where[i] for i in range(5))
    for dy in range(2):
        for position in range(4):
            held[dy, position] = right[dy * 4 + position][...]
    total = jnp.zeros((TILE, TILE), jnp.float32)
    for dy in range(2):
        for position in range(4):
            row = lax.rem(yh + dy + yl, 2)
            col = place(z + ahead(position, core) - x, core)
            total += nn(left[dy * 4 + position][...], held[row, col])
    mine[...] = total[:BLOCK]
    theirs[:, :BLOCK] = total[BLOCK:, BLOCK:].astype(theirs.dtype)
    theirs[:, BLOCK:] = total[BLOCK:, :BLOCK].astype(theirs.dtype)


def apply_kernel(other_rows, where, *rest):
    mixing, blocks, rest = rest[:8], rest[8:16], rest[16:]
    out, held = rest[-2:]
    x, yh, core, yl, z = (where[i] for i in range(5))

    @pl.when(pl.program_id(0) == 0)
    def _():
        which = lax.rem(yh + yl + int(other_rows), 2)
        for dy in range(2):

            @pl.when(which == dy)
            def _():
                for position in range(4):
                    col = place(z + ahead(position, core) - x, core)
                    held[col] = mixing[dy * 4 + position][...]

    total = jnp.zeros(out.shape, jnp.float32)
    for position in range(4):
        for half in range(2):
            total += nn(
                held[position, :, half * BLOCK : (half + 1) * BLOCK], blocks[position * 2 + half][...]
            )
    if not other_rows:
        total = total + linear_coef * rest[0][...].astype(jnp.float32)
    out[...] = total.astype(out.dtype)


def params(mib):
    return pltpu.CompilerParams(vmem_limit_bytes=mib * MIB)


def smem():
    return pl.BlockSpec(memory_space=pltpu.SMEM)


def whole():
    return pl.BlockSpec(memory_space=pltpu.VMEM)


def cost(flops, moved):
    return pl.CostEstimate(flops=flops, bytes_accessed=moved, transcendentals=0)


def gram_tiles(where, own, other, fore, fore_other, back, back_other, far, far_other, across):
    depth = own.shape[1]
    chunk = 512
    steps = depth // chunk
    block = lambda: pl.BlockSpec((BLOCK, chunk), lambda k: (0, k))
    full = lambda shape: pl.BlockSpec(shape, lambda k: (0,) * len(shape))
    near = pl.pallas_call(
        gram_near_kernel,
        grid=(steps,),
        in_specs=[block() for _ in range(7)],
        out_specs=full((2, 3, BLOCK, TILE)),
        out_shape=jax.ShapeDtypeStruct((2, 3, BLOCK, TILE), jnp.bfloat16),
        scratch_shapes=[pltpu.VMEM((2, 3, BLOCK, TILE), jnp.float32)],
        compiler_params=params(32),
        cost_estimate=cost(2 * 6 * BLOCK * TILE * depth, 7 * BLOCK * depth * 2 + 6 * BLOCK * TILE * 2),
        name="gram_near",
    )(own, other, fore, fore_other, back, back_other, across)
    return pl.pallas_call(
        gram_far_kernel,
        grid=(steps,),
        in_specs=[smem()] + [block() for _ in range(4)] + [full((2, 3, BLOCK, TILE))],
        out_specs=[full((BLOCK, TILE)) for _ in range(8)],
        out_shape=[jax.ShapeDtypeStruct((BLOCK, TILE), jnp.bfloat16) for _ in range(8)],
        scratch_shapes=[
            pltpu.VMEM((2, BLOCK, TILE), jnp.float32),
            pltpu.VMEM((2, 4, BLOCK, TILE), jnp.bfloat16),
        ],
        compiler_params=params(32),
        cost_estimate=cost(2 * 2 * BLOCK * TILE * depth, 4 * BLOCK * depth * 2 + 14 * BLOCK * TILE * 2),
        name="gram_far",
    )(where, own, across, far, far_other, near)


def square_part(where, left, right):
    return pl.pallas_call(
        square_kernel,
        in_specs=[smem()] + [whole() for _ in range(16)],
        out_specs=[whole(), whole()],
        out_shape=[
            jax.ShapeDtypeStruct((BLOCK, TILE), jnp.float32),
            jax.ShapeDtypeStruct((BLOCK, TILE), jnp.bfloat16),
        ],
        scratch_shapes=[pltpu.VMEM((2, 4, BLOCK, TILE), jnp.bfloat16)],
        compiler_params=params(32),
        cost_estimate=cost(2 * 8 * TILE * TILE * BLOCK, 16 * BLOCK * TILE * 2),
        name="square_part",
    )(where, *left, *right)


def apply_part(other_rows, where, mixing, blocks, own):
    depth = own.shape[1]
    chunk = 512
    column = lambda: pl.BlockSpec((BLOCK, chunk), lambda k: (0, k))
    full = lambda shape: pl.BlockSpec(shape, lambda k: (0,) * len(shape))
    extra = [] if other_rows else [own]
    return pl.pallas_call(
        functools.partial(apply_kernel, other_rows),
        grid=(depth // chunk,),
        in_specs=[smem()] + [full((BLOCK, TILE)) for _ in range(8)] + [column() for _ in range(8 + len(extra))],
        out_specs=column(),
        out_shape=jax.ShapeDtypeStruct((BLOCK, depth), jnp.bfloat16 if other_rows else jnp.float32),
        scratch_shapes=[pltpu.VMEM((4, BLOCK, TILE), jnp.bfloat16)],
        compiler_params=params(32),
        cost_estimate=cost(2 * 8 * BLOCK * BLOCK * depth, 9 * BLOCK * depth * 2 + 8 * BLOCK * TILE * 2),
        name="apply_other" if other_rows else "apply_own",
    )(where, *mixing, *blocks, *extra)


def on_device(iterate):
    total_cols = iterate.shape[1] * lax.axis_size("col")
    row, col = lax.axis_index("row"), lax.axis_index("col")
    where = jnp.stack([row // 4, row // 2 % 2, row % 2, col // 4, col % 4]).astype(jnp.int32)

    fore = send(iterate, "x_fore")
    back = send(iterate, "x_back")
    across = send(iterate, "yh")
    other = send(iterate, "core")
    far = send(fore, "x_fore")
    fore_other, back_other = send(back, "core"), send(fore, "core")
    far_other = send(far, "core")

    tiles = gram_tiles(
        where, iterate, other, fore, fore_other, back, back_other, far, far_other, across
    )
    total = tiles[0].astype(jnp.float32)
    for tile, slot in zip(tiles[1:], SLOTS[1:]):
        total = total + send(tile, slot).astype(jnp.float32)
    gram = total.astype(jnp.bfloat16)

    row_part = jnp.concatenate([gram[:, :BLOCK], send(gram[:, BLOCK:], "core")], axis=0)
    left = gather_ring(row_part, "z", "yh")
    right = gather_ring(gram, "x", "yl")
    mine, theirs = square_part(where, left, right)
    square = mine + send(theirs, "core").astype(jnp.float32)
    mixing = (cubic_coef * gram.astype(jnp.float32) + quintic_coef * square).astype(jnp.bfloat16)

    pieces = gather_even(mixing, "z", "yl")
    blocks = [iterate, other, fore, fore_other, back, back_other, far, far_other]
    applied_other = apply_part(True, where, pieces, blocks, iterate)
    applied = apply_part(False, where, pieces, blocks, iterate)
    update = applied + send(applied_other, "yh").astype(jnp.float32)
    return (math.sqrt(total_cols) * update).astype(jnp.bfloat16)


def gather_ring(value, ring, pair):
    there = send(value, pair)
    fore, back = send(value, ring + "_fore"), send(value, ring + "_back")
    there_fore, there_back = send(there, ring + "_fore"), send(there, ring + "_back")
    far = send(jnp.concatenate([fore, there_fore], axis=0), ring + "_fore")
    count = value.shape[0]
    return [value, fore, back, far[:count], there, there_fore, there_back, far[count:]]


def gather_even(value, ring, pair):
    fore, back = send(value, ring + "_fore"), send(value, ring + "_back")
    there = send(value, pair)
    far = send(fore, ring + "_fore")
    there_fore = send(there, ring + "_fore")
    there_back = send(back, pair)
    there_far = send(there_fore, ring + "_fore")
    return [value, fore, back, far, there, there_fore, there_back, there_far]


def solution(mesh):
    return jax.shard_map(
        on_device,
        mesh=mesh,
        in_specs=(P("row", "col"),),
        out_specs=P("row", "col"),
        check_vma=False,
    )
```

```python
import functools
import math

import jax
import jax.numpy as jnp
from jax import lax
from jax.experimental import pallas as pl
from jax.experimental.pallas import tpu as pltpu
from jax.sharding import PartitionSpec as P

linear_coef = 3.4445
cubic_coef = -4.775
quintic_coef = 2.0315

NX, NY, NC, NZ = 4, 2, 2, 4
BLOCK = 256
TILE = 2 * BLOCK
MIB = 1 << 20


def pairs(move):
    out = []
    for x in range(NX):
        for yh in range(NY):
            for core in range(NC):
                for yl in range(NY):
                    for z in range(NZ):
                        source = ((x * 2 + yh) * 2 + core) * 8 + yl * 4 + z
                        a, b, c, d, e = move(x, yh, core, yl, z)
                        a, e = a % NX, e % NZ
                        out.append((source, ((a * 2 + b) * 2 + c) * 8 + d * 4 + e))
    return out


def way(core):
    return 1 - 2 * core


MOVES = {
    "core": lambda x, yh, c, yl, z: (x, yh, 1 - c, yl, z),
    "yh": lambda x, yh, c, yl, z: (x, 1 - yh, c, yl, z),
    "yl": lambda x, yh, c, yl, z: (x, yh, c, 1 - yl, z),
    "x_fore": lambda x, yh, c, yl, z: (x + way(c), yh, c, yl, z),
    "x_back": lambda x, yh, c, yl, z: (x - way(c), yh, c, yl, z),
    "z_fore": lambda x, yh, c, yl, z: (x, yh, c, yl, z + way(c)),
    "z_back": lambda x, yh, c, yl, z: (x, yh, c, yl, z - way(c)),
}


def send(value, move):
    return lax.ppermute(value, ("row", "col"), pairs(MOVES[move]))


def place(delta, core):
    delta = lax.rem(delta + 8, 4)
    side = jnp.where(delta == 3 - 2 * core, 1, 2)
    return jnp.where(delta == 0, 0, jnp.where(delta == 2, 3, side))


def ahead(position, core):
    return (0, 2 * core - 1, 1 - 2 * core, 2)[position]


def nt(left, right):
    return lax.dot_general(left, right, (((1,), (1,)), ((), ())), preferred_element_type=jnp.float32)


def nn(left, right):
    return lax.dot_general(left, right, (((1,), (0,)), ((), ())), preferred_element_type=jnp.float32)


def gram_near_kernel(own, other, fore, fore_other, back, back_other, across, out):
    for r, rows in enumerate((own, across)):
        for q, cols in enumerate((own, other, fore, fore_other, back, back_other)):
            part = nt(rows[...], cols[...])
            out[r, q // 2, :, (q % 2) * BLOCK : (q % 2 + 1) * BLOCK] = part.astype(out.dtype)


def gram_far_kernel(where, own, across, far, far_other, near, *rest):
    outs, tiles = rest[:8], rest[8]
    x, yh, core, yl, z = (where[i] for i in range(5))
    for r, rows in enumerate((own, across)):
        for q, cols in enumerate((far, far_other)):
            tiles[r, :, q * BLOCK : (q + 1) * BLOCK] = nt(rows[...], cols[...]).astype(tiles.dtype)
    for index, out in enumerate(outs):
        dy, position = index // 4, index % 4
        row = lax.rem(yl + dy + yh, 2)
        col = place(z + ahead(position, core) - x, core)

        @pl.when(col == 3)
        def _():
            out[...] = tiles[row]

        @pl.when(col != 3)
        def _():
            out[...] = near[row, jnp.minimum(col, 2)]


def square_kernel(where, *rest):
    left, right, (mine, theirs), (held,) = rest[:8], rest[8:16], rest[16:18], rest[18:]
    x, yh, core, yl, z = (where[i] for i in range(5))
    for dy in range(2):
        for position in range(4):
            held[dy, position] = right[dy * 4 + position][...]
    total = jnp.zeros((TILE, TILE), jnp.float32)
    for dy in range(2):
        for position in range(4):
            row = lax.rem(yh + dy + yl, 2)
            col = place(z + ahead(position, core) - x, core)
            total += nn(left[dy * 4 + position][...], held[row, col])
    mine[...] = total[:BLOCK]
    theirs[:, :BLOCK] = total[BLOCK:, BLOCK:].astype(theirs.dtype)
    theirs[:, BLOCK:] = total[BLOCK:, :BLOCK].astype(theirs.dtype)


def apply_kernel(other_rows, where, *rest):
    mixing, blocks, rest = rest[:8], rest[8:16], rest[16:]
    out, held = rest[-2:]
    x, yh, core, yl, z = (where[i] for i in range(5))
    which = lax.rem(yh + yl + int(other_rows), 2)
    for dy in range(2):

        @pl.when(which == dy)
        def _():
            for position in range(4):
                col = place(z + ahead(position, core) - x, core)
                held[col] = mixing[dy * 4 + position][...]

    for start in range(0, out.shape[1], TILE):
        columns = slice(start, start + TILE)
        total = jnp.zeros((BLOCK, TILE), jnp.float32)
        for position in range(4):
            for half in range(2):
                total += nn(
                    held[position, :, half * BLOCK : (half + 1) * BLOCK],
                    blocks[position * 2 + half][:, columns],
                )
        if not other_rows:
            total = total + linear_coef * blocks[0][:, columns].astype(jnp.float32)
        out[:, columns] = total.astype(out.dtype)


def params(mib):
    return pltpu.CompilerParams(vmem_limit_bytes=mib * MIB)


def smem():
    return pl.BlockSpec(memory_space=pltpu.SMEM)


def whole():
    return pl.BlockSpec(memory_space=pltpu.VMEM)


def cost(flops, moved):
    return pl.CostEstimate(flops=flops, bytes_accessed=moved, transcendentals=0)


def gram_near(own, other, fore, fore_other, back, back_other, across):
    depth = own.shape[1]
    return pl.pallas_call(
        gram_near_kernel,
        in_specs=[whole() for _ in range(7)],
        out_specs=whole(),
        out_shape=jax.ShapeDtypeStruct((2, 3, BLOCK, TILE), jnp.bfloat16),
        compiler_params=params(24),
        cost_estimate=cost(2 * 6 * BLOCK * TILE * depth, 7 * BLOCK * depth * 2 + 6 * BLOCK * TILE * 2),
        name="gram_near",
    )(own, other, fore, fore_other, back, back_other, across)


def gram_far(where, own, across, far, far_other, near):
    depth = own.shape[1]
    return pl.pallas_call(
        gram_far_kernel,
        in_specs=[smem()] + [whole() for _ in range(5)],
        out_specs=[whole() for _ in range(8)],
        out_shape=[jax.ShapeDtypeStruct((BLOCK, TILE), jnp.bfloat16) for _ in range(8)],
        scratch_shapes=[pltpu.VMEM((2, BLOCK, TILE), jnp.bfloat16)],
        compiler_params=params(24),
        cost_estimate=cost(2 * 2 * BLOCK * TILE * depth, 4 * BLOCK * depth * 2 + 14 * BLOCK * TILE * 2),
        name="gram_far",
    )(where, own, across, far, far_other, near)


def square_part(where, left, right):
    return pl.pallas_call(
        square_kernel,
        in_specs=[smem()] + [whole() for _ in range(16)],
        out_specs=[whole(), whole()],
        out_shape=[
            jax.ShapeDtypeStruct((BLOCK, TILE), jnp.float32),
            jax.ShapeDtypeStruct((BLOCK, TILE), jnp.bfloat16),
        ],
        scratch_shapes=[pltpu.VMEM((2, 4, BLOCK, TILE), jnp.bfloat16)],
        compiler_params=params(24),
        cost_estimate=cost(2 * 8 * TILE * TILE * BLOCK, 16 * BLOCK * TILE * 2),
        name="square_part",
    )(where, *left, *right)


def apply_part(other_rows, where, mixing, blocks):
    depth = blocks[0].shape[1]
    return pl.pallas_call(
        functools.partial(apply_kernel, other_rows),
        in_specs=[smem()] + [whole() for _ in range(16)],
        out_specs=whole(),
        out_shape=jax.ShapeDtypeStruct((BLOCK, depth), jnp.bfloat16 if other_rows else jnp.float32),
        scratch_shapes=[pltpu.VMEM((4, BLOCK, TILE), jnp.bfloat16)],
        compiler_params=params(24),
        cost_estimate=cost(2 * 8 * BLOCK * BLOCK * depth, 9 * BLOCK * depth * 2 + 8 * BLOCK * TILE * 2),
        name="apply_other" if other_rows else "apply_own",
    )(where, *mixing, *blocks)


def add(left, right):
    return (left.astype(jnp.float32) + right.astype(jnp.float32)).astype(jnp.bfloat16)


def gather_rings(sides):
    first = [
        [send(value, pair), send(value, ring + "_fore"), send(value, ring + "_back")]
        for value, ring, pair in sides
    ]
    first = lax.optimization_barrier(first)
    second = [
        [
            send(jnp.concatenate([there, fore], axis=0), ring + "_fore"),
            send(there, ring + "_back"),
        ]
        for (there, fore, back), (value, ring, pair) in zip(first, sides)
    ]
    second = lax.optimization_barrier(second)
    out = []
    for (there, fore, back), (both, there_back), (value, ring, pair) in zip(first, second, sides):
        count = value.shape[0]
        there_fore, far = both[:count], both[count:]
        there_far = send(there_fore, ring + "_fore")
        out.append([value, fore, back, far, there, there_fore, there_back, there_far])
    return out


def gather_even(value, ring, pair):
    there, fore, back = lax.optimization_barrier(
        [send(value, pair), send(value, ring + "_fore"), send(value, ring + "_back")]
    )
    there_fore = send(there, ring + "_fore")
    far = send(fore, ring + "_fore")
    there_back = send(back, pair)
    there_far = send(there_fore, ring + "_fore")
    return [value, fore, back, far, there, there_fore, there_back, there_far]


def sum_over_col(tiles):
    chain = add(tiles[5], send(tiles[7], "z_back"))
    back = add(tiles[1], send(tiles[3], "z_back"))
    fore = add(tiles[2], send(tiles[6], "yl"))
    there = add(tiles[4], send(chain, "z_back"))
    total = tiles[0].astype(jnp.float32)
    total = total + send(back, "z_back").astype(jnp.float32)
    total = total + send(fore, "z_fore").astype(jnp.float32)
    total = total + send(there, "yl").astype(jnp.float32)
    return total.astype(jnp.bfloat16)


def on_device(iterate):
    total_cols = iterate.shape[1] * lax.axis_size("col")
    row, col = lax.axis_index("row"), lax.axis_index("col")
    where = jnp.stack([row >> 2, (row >> 1) & 1, row & 1, col >> 2, col & 3]).astype(jnp.int32)

    fore, back, across, other = lax.optimization_barrier(
        [send(iterate, move) for move in ("x_fore", "x_back", "yh", "core")]
    )
    far = send(fore, "x_fore")
    fore_other, back_other = send(back, "core"), send(fore, "core")
    near = gram_near(iterate, other, fore, fore_other, back, back_other, across)
    far_other = send(far, "core")
    gram = sum_over_col(gram_far(where, iterate, across, far, far_other, near))

    row_part = jnp.concatenate([gram[:, :BLOCK], send(gram[:, BLOCK:], "core")], axis=0)
    left, right = gather_rings([(row_part, "z", "yh"), (gram, "x", "yl")])
    mine, theirs = square_part(where, left, right)
    square = mine + send(theirs, "core").astype(jnp.float32)
    mixing = (cubic_coef * gram.astype(jnp.float32) + quintic_coef * square).astype(jnp.bfloat16)

    pieces = gather_even(mixing, "z", "yl")
    blocks = [iterate, other, fore, fore_other, back, back_other, far, far_other]
    applied_other = apply_part(True, where, pieces, blocks)
    applied = apply_part(False, where, pieces, blocks)
    update = applied + send(applied_other, "yh").astype(jnp.float32)
    return (math.sqrt(total_cols) * update).astype(jnp.bfloat16)


def solution(mesh):
    return jax.shard_map(
        on_device,
        mesh=mesh,
        in_specs=(P("row", "col"),),
        out_specs=P("row", "col"),
        check_vma=False,
    )
```

```python
import functools
import math

import jax
import jax.numpy as jnp
from jax import lax
from jax.experimental import pallas as pl
from jax.experimental.pallas import tpu as pltpu
from jax.sharding import PartitionSpec as P

linear_coef = 3.4445
cubic_coef = -4.775
quintic_coef = 2.0315

NX, NY, NC, NZ = 4, 2, 2, 4
BLOCK = 256
TILE = 2 * BLOCK
MIB = 1 << 20


def pairs(move):
    out = []
    for x in range(NX):
        for yh in range(NY):
            for core in range(NC):
                for yl in range(NY):
                    for z in range(NZ):
                        source = ((x * 2 + yh) * 2 + core) * 8 + yl * 4 + z
                        a, b, c, d, e = move(x, yh, core, yl, z)
                        a, e = a % NX, e % NZ
                        out.append((source, ((a * 2 + b) * 2 + c) * 8 + d * 4 + e))
    return out


def way(core):
    return 1 - 2 * core


MOVES = {
    "core": lambda x, yh, c, yl, z: (x, yh, 1 - c, yl, z),
    "yh": lambda x, yh, c, yl, z: (x, 1 - yh, c, yl, z),
    "yl": lambda x, yh, c, yl, z: (x, yh, c, 1 - yl, z),
    "x_fore": lambda x, yh, c, yl, z: (x + way(c), yh, c, yl, z),
    "x_back": lambda x, yh, c, yl, z: (x - way(c), yh, c, yl, z),
    "z_fore": lambda x, yh, c, yl, z: (x, yh, c, yl, z + way(c)),
    "z_back": lambda x, yh, c, yl, z: (x, yh, c, yl, z - way(c)),
}


def send(value, move):
    return lax.ppermute(value, ("row", "col"), pairs(MOVES[move]))


def place(delta, core):
    delta = lax.rem(delta + 8, 4)
    side = jnp.where(delta == 3 - 2 * core, 1, 2)
    return jnp.where(delta == 0, 0, jnp.where(delta == 2, 3, side))


def ahead(position, core):
    return (0, 2 * core - 1, 1 - 2 * core, 2)[position]


def nt(left, right):
    return lax.dot_general(left, right, (((1,), (1,)), ((), ())), preferred_element_type=jnp.float32)


def nn(left, right):
    return lax.dot_general(left, right, (((1,), (0,)), ((), ())), preferred_element_type=jnp.float32)


def gram_near_kernel(own, other, fore, fore_other, back, back_other, across, out):
    for r, rows in enumerate((own, across)):
        for q, cols in enumerate((own, other, fore, fore_other, back, back_other)):
            part = nt(rows[...], cols[...])
            out[r, q // 2, :, (q % 2) * BLOCK : (q % 2 + 1) * BLOCK] = part.astype(out.dtype)


def gram_far_own_kernel(own, across, far, out):
    for r, rows in enumerate((own, across)):
        out[r] = nt(rows[...], far[...]).astype(out.dtype)


def gram_far_kernel(where, own, across, far_other, far_own, near, *rest):
    outs, tiles = rest[:8], rest[8]
    x, yh, core, yl, z = (where[i] for i in range(5))
    for r, rows in enumerate((own, across)):
        tiles[r, :, :BLOCK] = far_own[r]
        tiles[r, :, BLOCK:] = nt(rows[...], far_other[...]).astype(tiles.dtype)
    for index, out in enumerate(outs):
        dy, position = index // 4, index % 4
        row = lax.rem(yl + dy + yh, 2)
        col = place(z + ahead(position, core) - x, core)

        @pl.when(col == 3)
        def _():
            out[...] = tiles[row]

        @pl.when(col != 3)
        def _():
            out[...] = near[row, jnp.minimum(col, 2)]


def square_kernel(where, *rest):
    left, right, (mine, theirs), (held,) = rest[:8], rest[8:16], rest[16:18], rest[18:]
    x, yh, core, yl, z = (where[i] for i in range(5))
    for dy in range(2):
        for position in range(4):
            held[dy, position] = right[dy * 4 + position][...]
    total = jnp.zeros((TILE, TILE), jnp.float32)
    for dy in range(2):
        for position in range(4):
            row = lax.rem(yh + dy + yl, 2)
            col = place(z + ahead(position, core) - x, core)
            total += nn(left[dy * 4 + position][...], held[row, col])
    mine[...] = total[:BLOCK]
    theirs[:, :BLOCK] = total[BLOCK:, BLOCK:].astype(theirs.dtype)
    theirs[:, BLOCK:] = total[BLOCK:, :BLOCK].astype(theirs.dtype)


def apply_kernel(other_rows, where, *rest):
    mixing, blocks, rest = rest[:8], rest[8:16], rest[16:]
    out, held = rest[-2:]
    x, yh, core, yl, z = (where[i] for i in range(5))
    which = lax.rem(yh + yl + int(other_rows), 2)
    for dy in range(2):

        @pl.when(which == dy)
        def _():
            for position in range(4):
                col = place(z + ahead(position, core) - x, core)
                held[col] = mixing[dy * 4 + position][...]

    for start in range(0, out.shape[1], TILE):
        columns = slice(start, start + TILE)
        total = jnp.zeros((BLOCK, TILE), jnp.float32)
        for position in range(4):
            for half in range(2):
                total += nn(
                    held[position, :, half * BLOCK : (half + 1) * BLOCK],
                    blocks[position * 2 + half][:, columns],
                )
        if not other_rows:
            total = total + linear_coef * blocks[0][:, columns].astype(jnp.float32)
        out[:, columns] = total.astype(out.dtype)


def params(mib):
    return pltpu.CompilerParams(vmem_limit_bytes=mib * MIB)


def smem():
    return pl.BlockSpec(memory_space=pltpu.SMEM)


def whole():
    return pl.BlockSpec(memory_space=pltpu.VMEM)


def cost(flops, moved):
    return pl.CostEstimate(flops=flops, bytes_accessed=moved, transcendentals=0)


def gram_near(own, other, fore, fore_other, back, back_other, across):
    depth = own.shape[1]
    return pl.pallas_call(
        gram_near_kernel,
        in_specs=[whole() for _ in range(7)],
        out_specs=whole(),
        out_shape=jax.ShapeDtypeStruct((2, 3, BLOCK, TILE), jnp.bfloat16),
        compiler_params=params(24),
        cost_estimate=cost(2 * 6 * BLOCK * TILE * depth, 7 * BLOCK * depth * 2 + 6 * BLOCK * TILE * 2),
        name="gram_near",
    )(own, other, fore, fore_other, back, back_other, across)


def gram_far_own(own, across, far):
    depth = own.shape[1]
    return pl.pallas_call(
        gram_far_own_kernel,
        in_specs=[whole() for _ in range(3)],
        out_specs=whole(),
        out_shape=jax.ShapeDtypeStruct((2, BLOCK, BLOCK), jnp.bfloat16),
        compiler_params=params(24),
        cost_estimate=cost(2 * 2 * BLOCK * BLOCK * depth, 3 * BLOCK * depth * 2 + 2 * BLOCK * BLOCK * 2),
        name="gram_far_own",
    )(own, across, far)


def gram_far(where, own, across, far_other, far_own, near):
    depth = own.shape[1]
    return pl.pallas_call(
        gram_far_kernel,
        in_specs=[smem()] + [whole() for _ in range(5)],
        out_specs=[whole() for _ in range(8)],
        out_shape=[jax.ShapeDtypeStruct((BLOCK, TILE), jnp.bfloat16) for _ in range(8)],
        scratch_shapes=[pltpu.VMEM((2, BLOCK, TILE), jnp.bfloat16)],
        compiler_params=params(24),
        cost_estimate=cost(2 * 2 * BLOCK * BLOCK * depth, 3 * BLOCK * depth * 2 + 15 * BLOCK * TILE * 2),
        name="gram_far",
    )(where, own, across, far_other, far_own, near)


def square_part(where, left, right):
    return pl.pallas_call(
        square_kernel,
        in_specs=[smem()] + [whole() for _ in range(16)],
        out_specs=[whole(), whole()],
        out_shape=[
            jax.ShapeDtypeStruct((BLOCK, TILE), jnp.float32),
            jax.ShapeDtypeStruct((BLOCK, TILE), jnp.bfloat16),
        ],
        scratch_shapes=[pltpu.VMEM((2, 4, BLOCK, TILE), jnp.bfloat16)],
        compiler_params=params(24),
        cost_estimate=cost(2 * 8 * TILE * TILE * BLOCK, 16 * BLOCK * TILE * 2),
        name="square_part",
    )(where, *left, *right)


def apply_part(other_rows, where, mixing, blocks):
    depth = blocks[0].shape[1]
    return pl.pallas_call(
        functools.partial(apply_kernel, other_rows),
        in_specs=[smem()] + [whole() for _ in range(16)],
        out_specs=whole(),
        out_shape=jax.ShapeDtypeStruct((BLOCK, depth), jnp.bfloat16 if other_rows else jnp.float32),
        scratch_shapes=[pltpu.VMEM((4, BLOCK, TILE), jnp.bfloat16)],
        compiler_params=params(24),
        cost_estimate=cost(2 * 8 * BLOCK * BLOCK * depth, 9 * BLOCK * depth * 2 + 8 * BLOCK * TILE * 2),
        name="apply_other" if other_rows else "apply_own",
    )(where, *mixing, *blocks)


def add(left, right):
    return (left.astype(jnp.float32) + right.astype(jnp.float32)).astype(jnp.bfloat16)


def gather_rings(sides):
    first = [
        [send(value, ring + "_back"), send(value, ring + "_fore"), send(value, pair)]
        for value, ring, pair in sides
    ]
    first = lax.optimization_barrier(first)
    second = [
        [
            send(there, ring + "_back"),
            send(jnp.concatenate([there, fore], axis=0), ring + "_fore"),
        ]
        for (back, fore, there), (value, ring, pair) in zip(first, sides)
    ]
    second = lax.optimization_barrier(second)
    out = []
    for (back, fore, there), (there_back, both), (value, ring, pair) in zip(first, second, sides):
        count = value.shape[0]
        there_fore, far = both[:count], both[count:]
        there_far = send(there_fore, ring + "_fore")
        out.append([value, fore, back, far, there, there_fore, there_back, there_far])
    return out


def gather_even(value, ring, pair):
    fore, back = send(value, ring + "_fore"), send(value, ring + "_back")
    there = send(value, pair)
    far = send(fore, ring + "_fore")
    there_fore = send(there, ring + "_fore")
    there_back = send(back, pair)
    there_far = send(there_fore, ring + "_fore")
    return [value, fore, back, far, there, there_fore, there_back, there_far]


def sum_over_col(tiles):
    chain = add(tiles[5], send(tiles[7], "z_back"))
    back = add(tiles[1], send(tiles[3], "z_back"))
    fore = add(tiles[2], send(tiles[6], "yl"))
    there = add(tiles[4], send(chain, "z_back"))
    total = tiles[0].astype(jnp.float32)
    total = total + send(back, "z_back").astype(jnp.float32)
    total = total + send(fore, "z_fore").astype(jnp.float32)
    total = total + send(there, "yl").astype(jnp.float32)
    return total.astype(jnp.bfloat16)


def on_device(iterate):
    total_cols = iterate.shape[1] * lax.axis_size("col")
    row, col = lax.axis_index("row"), lax.axis_index("col")
    where = jnp.stack([row >> 2, (row >> 1) & 1, row & 1, col >> 2, col & 3]).astype(jnp.int32)

    other, across, back, fore = lax.optimization_barrier(
        [send(iterate, move) for move in ("core", "yh", "x_back", "x_fore")]
    )
    fore_other, back_other = send(back, "core"), send(fore, "core")
    far = send(fore, "x_fore")
    near = gram_near(iterate, other, fore, fore_other, back, back_other, across)
    far, near = lax.optimization_barrier((far, near))
    far_other = send(far, "core")
    far_own = gram_far_own(iterate, across, far)
    gram = sum_over_col(gram_far(where, iterate, across, far_other, far_own, near))

    row_part = jnp.concatenate([gram[:, :BLOCK], send(gram[:, BLOCK:], "core")], axis=0)
    left, right = gather_rings([(row_part, "z", "yh"), (gram, "x", "yl")])
    mine, theirs = square_part(where, left, right)
    square = mine + send(theirs, "core").astype(jnp.float32)
    mixing = (cubic_coef * gram.astype(jnp.float32) + quintic_coef * square).astype(jnp.bfloat16)

    pieces = gather_even(mixing, "z", "yl")
    blocks = [iterate, other, fore, fore_other, back, back_other, far, far_other]
    applied_other = apply_part(True, where, pieces, blocks)
    applied = apply_part(False, where, pieces, blocks)
    update = applied + send(applied_other, "yh").astype(jnp.float32)
    return (math.sqrt(total_cols) * update).astype(jnp.bfloat16)


def solution(mesh):
    return jax.shard_map(
        on_device,
        mesh=mesh,
        in_specs=(P("row", "col"),),
        out_specs=P("row", "col"),
        check_vma=False,
    )
```

```python
import functools
import math

import jax
import jax.numpy as jnp
from jax import lax
from jax.experimental import pallas as pl
from jax.experimental.pallas import tpu as pltpu
from jax.sharding import PartitionSpec as P

linear_coef = 3.4445
cubic_coef = -4.775
quintic_coef = 2.0315

NX, NY, NC, NZ = 4, 2, 2, 4
BLOCK = 256
TILE = 2 * BLOCK
MIB = 1 << 20


def pairs(move):
    out = []
    for x in range(NX):
        for yh in range(NY):
            for core in range(NC):
                for yl in range(NY):
                    for z in range(NZ):
                        source = ((x * 2 + yh) * 2 + core) * 8 + yl * 4 + z
                        a, b, c, d, e = move(x, yh, core, yl, z)
                        a, e = a % NX, e % NZ
                        out.append((source, ((a * 2 + b) * 2 + c) * 8 + d * 4 + e))
    return out


def way(core):
    return 1 - 2 * core


MOVES = {
    "core": lambda x, yh, c, yl, z: (x, yh, 1 - c, yl, z),
    "yh": lambda x, yh, c, yl, z: (x, 1 - yh, c, yl, z),
    "yl": lambda x, yh, c, yl, z: (x, yh, c, 1 - yl, z),
    "x_fore": lambda x, yh, c, yl, z: (x + way(c), yh, c, yl, z),
    "x_back": lambda x, yh, c, yl, z: (x - way(c), yh, c, yl, z),
    "z_fore": lambda x, yh, c, yl, z: (x, yh, c, yl, z + way(c)),
    "z_back": lambda x, yh, c, yl, z: (x, yh, c, yl, z - way(c)),
}


def send(value, move):
    return lax.ppermute(value, ("row", "col"), pairs(MOVES[move]))


def place(delta, core):
    delta = lax.rem(delta + 8, 4)
    side = jnp.where(delta == 3 - 2 * core, 1, 2)
    return jnp.where(delta == 0, 0, jnp.where(delta == 2, 3, side))


def ahead(position, core):
    return (0, 2 * core - 1, 1 - 2 * core, 2)[position]


def nt(left, right):
    return lax.dot_general(left, right, (((1,), (1,)), ((), ())), preferred_element_type=jnp.float32)


def nn(left, right):
    return lax.dot_general(left, right, (((1,), (0,)), ((), ())), preferred_element_type=jnp.float32)


def gram_near_kernel(own, other, fore, fore_other, back, back_other, across, out):
    for r, rows in enumerate((own, across)):
        for q, cols in enumerate((own, other, fore, fore_other, back, back_other)):
            part = nt(rows[...], cols[...])
            out[r, q // 2, :, (q % 2) * BLOCK : (q % 2 + 1) * BLOCK] = part.astype(out.dtype)


def gram_far_own_kernel(own, across, far, out):
    for r, rows in enumerate((own, across)):
        out[r] = nt(rows[...], far[...]).astype(out.dtype)


def gram_far_kernel(where, own, across, far_other, far_own, near, *rest):
    outs, tiles = rest[:8], rest[8]
    x, yh, core, yl, z = (where[i] for i in range(5))
    for r, rows in enumerate((own, across)):
        tiles[r, :, :BLOCK] = far_own[r]
        tiles[r, :, BLOCK:] = nt(rows[...], far_other[...]).astype(tiles.dtype)
    for index, out in enumerate(outs):
        dy, position = index // 4, index % 4
        row = lax.rem(yl + dy + yh, 2)
        col = place(z + ahead(position, core) - x, core)

        @pl.when(col == 3)
        def _():
            out[...] = tiles[row]

        @pl.when(col != 3)
        def _():
            out[...] = near[row, jnp.minimum(col, 2)]


def square_kernel(where, *rest):
    left, right, (mine, theirs), (held,) = rest[:8], rest[8:16], rest[16:18], rest[18:]
    x, yh, core, yl, z = (where[i] for i in range(5))
    for dy in range(2):
        for position in range(4):
            held[dy, position] = right[dy * 4 + position][...]
    total = jnp.zeros((TILE, TILE), jnp.float32)
    for dy in range(2):
        for position in range(4):
            row = lax.rem(yh + dy + yl, 2)
            col = place(z + ahead(position, core) - x, core)
            total += nn(left[dy * 4 + position][...], held[row, col])
    mine[...] = total[:BLOCK]
    theirs[:, :BLOCK] = total[BLOCK:, BLOCK:].astype(theirs.dtype)
    theirs[:, BLOCK:] = total[BLOCK:, :BLOCK].astype(theirs.dtype)


def apply_kernel(other_rows, where, *rest):
    mixing, blocks, rest = rest[:8], rest[8:16], rest[16:]
    out, held = rest[-2:]
    x, yh, core, yl, z = (where[i] for i in range(5))
    which = lax.rem(yh + yl + int(other_rows), 2)
    for dy in range(2):

        @pl.when(which == dy)
        def _():
            for position in range(4):
                col = place(z + ahead(position, core) - x, core)
                held[col] = mixing[dy * 4 + position][...]

    for start in range(0, out.shape[1], TILE):
        columns = slice(start, start + TILE)
        total = jnp.zeros((BLOCK, TILE), jnp.float32)
        for position in range(4):
            for half in range(2):
                total += nn(
                    held[position, :, half * BLOCK : (half + 1) * BLOCK],
                    blocks[position * 2 + half][:, columns],
                )
        if not other_rows:
            total = total + linear_coef * blocks[0][:, columns].astype(jnp.float32)
        out[:, columns] = total.astype(out.dtype)


def params(mib):
    return pltpu.CompilerParams(vmem_limit_bytes=mib * MIB)


def smem():
    return pl.BlockSpec(memory_space=pltpu.SMEM)


def whole():
    return pl.BlockSpec(memory_space=pltpu.VMEM)


def cost(flops, moved):
    return pl.CostEstimate(flops=flops, bytes_accessed=moved, transcendentals=0)


def gram_near(own, other, fore, fore_other, back, back_other, across):
    depth = own.shape[1]
    return pl.pallas_call(
        gram_near_kernel,
        in_specs=[whole() for _ in range(7)],
        out_specs=whole(),
        out_shape=jax.ShapeDtypeStruct((2, 3, BLOCK, TILE), jnp.bfloat16),
        compiler_params=params(24),
        cost_estimate=cost(2 * 6 * BLOCK * TILE * depth, 7 * BLOCK * depth * 2 + 6 * BLOCK * TILE * 2),
        name="gram_near",
    )(own, other, fore, fore_other, back, back_other, across)


def gram_far_own(own, across, far):
    depth = own.shape[1]
    return pl.pallas_call(
        gram_far_own_kernel,
        in_specs=[whole() for _ in range(3)],
        out_specs=whole(),
        out_shape=jax.ShapeDtypeStruct((2, BLOCK, BLOCK), jnp.bfloat16),
        compiler_params=params(24),
        cost_estimate=cost(2 * 2 * BLOCK * BLOCK * depth, 3 * BLOCK * depth * 2 + 2 * BLOCK * BLOCK * 2),
        name="gram_far_own",
    )(own, across, far)


def gram_far(where, own, across, far_other, far_own, near):
    depth = own.shape[1]
    return pl.pallas_call(
        gram_far_kernel,
        in_specs=[smem()] + [whole() for _ in range(5)],
        out_specs=[whole() for _ in range(8)],
        out_shape=[jax.ShapeDtypeStruct((BLOCK, TILE), jnp.bfloat16) for _ in range(8)],
        scratch_shapes=[pltpu.VMEM((2, BLOCK, TILE), jnp.bfloat16)],
        compiler_params=params(24),
        cost_estimate=cost(2 * 2 * BLOCK * BLOCK * depth, 3 * BLOCK * depth * 2 + 15 * BLOCK * TILE * 2),
        name="gram_far",
    )(where, own, across, far_other, far_own, near)


def square_part(where, left, right):
    return pl.pallas_call(
        square_kernel,
        in_specs=[smem()] + [whole() for _ in range(16)],
        out_specs=[whole(), whole()],
        out_shape=[
            jax.ShapeDtypeStruct((BLOCK, TILE), jnp.float32),
            jax.ShapeDtypeStruct((BLOCK, TILE), jnp.bfloat16),
        ],
        scratch_shapes=[pltpu.VMEM((2, 4, BLOCK, TILE), jnp.bfloat16)],
        compiler_params=params(24),
        cost_estimate=cost(2 * 8 * TILE * TILE * BLOCK, 16 * BLOCK * TILE * 2),
        name="square_part",
    )(where, *left, *right)


def apply_part(other_rows, where, mixing, blocks):
    depth = blocks[0].shape[1]
    return pl.pallas_call(
        functools.partial(apply_kernel, other_rows),
        in_specs=[smem()] + [whole() for _ in range(16)],
        out_specs=whole(),
        out_shape=jax.ShapeDtypeStruct((BLOCK, depth), jnp.bfloat16 if other_rows else jnp.float32),
        scratch_shapes=[pltpu.VMEM((4, BLOCK, TILE), jnp.bfloat16)],
        compiler_params=params(24),
        cost_estimate=cost(2 * 8 * BLOCK * BLOCK * depth, 9 * BLOCK * depth * 2 + 8 * BLOCK * TILE * 2),
        name="apply_other" if other_rows else "apply_own",
    )(where, *mixing, *blocks)


def add(left, right):
    return (left.astype(jnp.float32) + right.astype(jnp.float32)).astype(jnp.bfloat16)


def gather_rings(sides):
    first = [
        [send(value, ring + "_back"), send(value, ring + "_fore"), send(value, pair)]
        for value, ring, pair in sides
    ]
    first = [lax.optimization_barrier(part) for part in first]
    second = [
        [
            send(there, ring + "_back"),
            send(jnp.concatenate([there, fore], axis=0), ring + "_fore"),
        ]
        for (back, fore, there), (value, ring, pair) in zip(first, sides)
    ]
    second = [lax.optimization_barrier(part) for part in second]
    out = []
    for (back, fore, there), (there_back, both), (value, ring, pair) in zip(first, second, sides):
        count = value.shape[0]
        there_fore, far = both[:count], both[count:]
        there_far = send(there_fore, ring + "_fore")
        out.append([value, fore, back, far, there, there_fore, there_back, there_far])
    return out


def gather_even(value, ring, pair):
    fore, back = send(value, ring + "_fore"), send(value, ring + "_back")
    there = send(value, pair)
    far = send(fore, ring + "_fore")
    there_fore = send(there, ring + "_fore")
    there_back = send(back, pair)
    there_far = send(there_fore, ring + "_fore")
    return [value, fore, back, far, there, there_fore, there_back, there_far]


def sum_over_col(tiles):
    chain = add(tiles[5], send(tiles[7], "z_back"))
    back = add(tiles[1], send(tiles[3], "z_back"))
    fore = add(tiles[2], send(tiles[6], "yl"))
    there = add(tiles[4], send(chain, "z_back"))
    total = tiles[0].astype(jnp.float32)
    total = total + send(back, "z_back").astype(jnp.float32)
    total = total + send(fore, "z_fore").astype(jnp.float32)
    total = total + send(there, "yl").astype(jnp.float32)
    return total.astype(jnp.bfloat16)


def on_device(iterate):
    total_cols = iterate.shape[1] * lax.axis_size("col")
    row, col = lax.axis_index("row"), lax.axis_index("col")
    where = jnp.stack([row >> 2, (row >> 1) & 1, row & 1, col >> 2, col & 3]).astype(jnp.int32)

    iterate, where = lax.optimization_barrier((iterate, where))
    other, across, back, fore = lax.optimization_barrier(
        [send(iterate, move) for move in ("core", "yh", "x_back", "x_fore")]
    )
    fore_other, back_other = send(back, "core"), send(fore, "core")
    far = send(fore, "x_fore")
    near = gram_near(iterate, other, fore, fore_other, back, back_other, across)
    far, near = lax.optimization_barrier((far, near))
    far_other = send(far, "core")
    far_own = gram_far_own(iterate, across, far)
    gram = sum_over_col(gram_far(where, iterate, across, far_other, far_own, near))

    row_part = jnp.concatenate([gram[:, :BLOCK], send(gram[:, BLOCK:], "core")], axis=0)
    left, right = gather_rings([(row_part, "z", "yh"), (gram, "x", "yl")])
    mine, theirs = square_part(where, left, right)
    square = mine + send(theirs, "core").astype(jnp.float32)
    mixing = (cubic_coef * gram.astype(jnp.float32) + quintic_coef * square).astype(jnp.bfloat16)

    pieces = gather_even(mixing, "z", "yl")
    blocks = [iterate, other, fore, fore_other, back, back_other, far, far_other]
    applied_other = apply_part(True, where, pieces, blocks)
    applied = apply_part(False, where, pieces, blocks)
    update = applied + send(applied_other, "yh").astype(jnp.float32)
    return (math.sqrt(total_cols) * update).astype(jnp.bfloat16)


def solution(mesh):
    return jax.shard_map(
        on_device,
        mesh=mesh,
        in_specs=(P("row", "col"),),
        out_specs=P("row", "col"),
        check_vma=False,
    )
```

```python
import functools
import math

import jax
import jax.numpy as jnp
from jax import lax
from jax.experimental import pallas as pl
from jax.experimental.pallas import tpu as pltpu
from jax.sharding import PartitionSpec as P

linear_coef = 3.4445
cubic_coef = -4.775
quintic_coef = 2.0315

NX, NY, NC, NZ = 4, 2, 2, 4
BLOCK = 256
TILE = 2 * BLOCK
MIB = 1 << 20


def pairs(move):
    out = []
    for x in range(NX):
        for yh in range(NY):
            for core in range(NC):
                for yl in range(NY):
                    for z in range(NZ):
                        source = ((x * 2 + yh) * 2 + core) * 8 + yl * 4 + z
                        a, b, c, d, e = move(x, yh, core, yl, z)
                        a, e = a % NX, e % NZ
                        out.append((source, ((a * 2 + b) * 2 + c) * 8 + d * 4 + e))
    return out


def way(core):
    return 1 - 2 * core


def mask(position, core):
    return (0, 1 + 2 * core, 3 - 2 * core, 2)[position]


MOVES = {
    "core": lambda x, yh, c, yl, z: (x, yh, 1 - c, yl, z),
    "yh": lambda x, yh, c, yl, z: (x, 1 - yh, c, yl, z),
    "yl": lambda x, yh, c, yl, z: (x, yh, c, 1 - yl, z),
    "x_fore": lambda x, yh, c, yl, z: (x + way(c), yh, c, yl, z),
    "x_back": lambda x, yh, c, yl, z: (x - way(c), yh, c, yl, z),
    "x_first": lambda x, yh, c, yl, z: (x ^ mask(1, c), yh, c, yl, z),
    "x_second": lambda x, yh, c, yl, z: (x ^ mask(2, c), yh, c, yl, z),
    "z_first": lambda x, yh, c, yl, z: (x, yh, c, yl, z ^ mask(1, c)),
    "z_second": lambda x, yh, c, yl, z: (x, yh, c, yl, z ^ mask(2, c)),
}


def send(value, move):
    return lax.ppermute(value, ("row", "col"), pairs(MOVES[move]))


def place(delta, core):
    delta = lax.rem(delta + 8, 4)
    side = jnp.where(delta == 3 - 2 * core, 1, 2)
    return jnp.where(delta == 0, 0, jnp.where(delta == 2, 3, side))


def partner(difference, core):
    side = jnp.where(difference == 1 + 2 * core, 1, 2)
    return jnp.where(difference == 0, 0, jnp.where(difference == 2, 3, side))


def nt(left, right):
    return lax.dot_general(left, right, (((1,), (1,)), ((), ())), preferred_element_type=jnp.float32)


def nn(left, right):
    return lax.dot_general(left, right, (((1,), (0,)), ((), ())), preferred_element_type=jnp.float32)


def gram_near_kernel(own, other, across, across_other, fore, back, out):
    for r, rows in enumerate((own, other, across, across_other)):
        for q, cols in enumerate((own, fore, back)):
            part = nt(rows[...], cols[...])
            out[r // 2, q, (r % 2) * BLOCK : (r % 2 + 1) * BLOCK] = part.astype(out.dtype)


def gram_far_kernel(where, own, other, across, across_other, far, near, *rest):
    outs, tiles = rest[:6], rest[6]
    x, yh, core, yl, z = (where[i] for i in range(5))
    for r, rows in enumerate((own, other, across, across_other)):
        part = nt(rows[...], far[...])
        tiles[r // 2, (r % 2) * BLOCK : (r % 2 + 1) * BLOCK] = part.astype(tiles.dtype)
    for index in range(8):
        dy, position = index // 4, index % 4
        row = lax.rem(yl + dy + yh, 2)
        col = place((z ^ mask(position, core)) - x, core)
        out, start = outs[dy * 3 + min(position, 2)], TILE * (position == 3)

        @pl.when(col == 3)
        def _():
            out[start : start + TILE] = tiles[row]

        @pl.when(col != 3)
        def _():
            out[start : start + TILE] = near[row, jnp.minimum(col, 2)]


def piece(refs, index):
    dy, position = index // 4, index % 4
    ref = refs[dy * 3 + min(position, 2)]
    if position < 2:
        return ref[...]
    count = ref.shape[0] // 2
    return ref[(position - 2) * count : (position - 1) * count]


def square_kernel(where, *rest):
    left, right, (mine, theirs), (held,) = rest[:6], rest[6:12], rest[12:14], rest[14:]
    x, yh, core, yl, z = (where[i] for i in range(5))
    for index in range(8):
        held[index // 4, index % 4] = piece(right, index)
    total = jnp.zeros((TILE, TILE), jnp.float32)
    for index in range(8):
        row = lax.rem(yh + index // 4 + yl, 2)
        col = partner(z ^ mask(index % 4, core) ^ x, core)
        total += nn(piece(left, index), held[row, col])
    mine[...] = total[:BLOCK]
    theirs[:, :BLOCK] = total[BLOCK:, BLOCK:].astype(theirs.dtype)
    theirs[:, BLOCK:] = total[BLOCK:, :BLOCK].astype(theirs.dtype)


def apply_kernel(other_rows, where, *rest):
    mixing, blocks, (out, held) = rest[:6], rest[6:14], rest[14:]
    x, yh, core, yl, z = (where[i] for i in range(5))
    which = lax.rem(yh + yl + int(other_rows), 2)
    for dy in range(2):

        @pl.when(which == dy)
        def _():
            for position in range(4):
                col = place((z ^ mask(position, core)) - x, core)
                held[col] = piece(mixing, dy * 4 + position)

    for start in range(0, out.shape[1], TILE):
        columns = slice(start, start + TILE)
        total = jnp.zeros((BLOCK, TILE), jnp.float32)
        for position in range(4):
            for half in range(2):
                total += nn(
                    held[position, :, half * BLOCK : (half + 1) * BLOCK],
                    blocks[position * 2 + half][:, columns],
                )
        if not other_rows:
            total = total + linear_coef * blocks[0][:, columns].astype(jnp.float32)
        out[:, columns] = total.astype(out.dtype)


def params(mib):
    return pltpu.CompilerParams(vmem_limit_bytes=mib * MIB)


def smem():
    return pl.BlockSpec(memory_space=pltpu.SMEM)


def whole():
    return pl.BlockSpec(memory_space=pltpu.VMEM)


def cost(flops, moved):
    return pl.CostEstimate(flops=flops, bytes_accessed=moved, transcendentals=0)


def gram_near(own, other, across, across_other, fore, back):
    depth = own.shape[1]
    return pl.pallas_call(
        gram_near_kernel,
        in_specs=[whole() for _ in range(6)],
        out_specs=whole(),
        out_shape=jax.ShapeDtypeStruct((2, 3, TILE, BLOCK), jnp.bfloat16),
        compiler_params=params(24),
        cost_estimate=cost(2 * 6 * BLOCK * TILE * depth, 6 * BLOCK * depth * 2 + 6 * BLOCK * TILE * 2),
        name="gram_near",
    )(own, other, across, across_other, fore, back)


def gram_far(where, own, other, across, across_other, far, near):
    depth = own.shape[1]
    shapes = [(TILE * (2 if position == 2 else 1), BLOCK) for _ in range(2) for position in range(3)]
    return pl.pallas_call(
        gram_far_kernel,
        in_specs=[smem()] + [whole() for _ in range(6)],
        out_specs=[whole() for _ in range(6)],
        out_shape=[jax.ShapeDtypeStruct(shape, jnp.bfloat16) for shape in shapes],
        scratch_shapes=[pltpu.VMEM((2, TILE, BLOCK), jnp.bfloat16)],
        compiler_params=params(24),
        cost_estimate=cost(2 * 2 * BLOCK * TILE * depth, 5 * BLOCK * depth * 2 + 14 * BLOCK * TILE * 2),
        name="gram_far",
    )(where, own, other, across, across_other, far, near)


def square_part(where, left, right):
    return pl.pallas_call(
        square_kernel,
        in_specs=[smem()] + [whole() for _ in range(12)],
        out_specs=[whole(), whole()],
        out_shape=[
            jax.ShapeDtypeStruct((BLOCK, TILE), jnp.float32),
            jax.ShapeDtypeStruct((BLOCK, TILE), jnp.bfloat16),
        ],
        scratch_shapes=[pltpu.VMEM((2, 4, BLOCK, TILE), jnp.bfloat16)],
        compiler_params=params(24),
        cost_estimate=cost(2 * 8 * TILE * TILE * BLOCK, 16 * BLOCK * TILE * 2),
        name="square_part",
    )(where, *left, *right)


def apply_part(other_rows, where, mixing, blocks):
    depth = blocks[0].shape[1]
    return pl.pallas_call(
        functools.partial(apply_kernel, other_rows),
        in_specs=[smem()] + [whole() for _ in range(14)],
        out_specs=whole(),
        out_shape=jax.ShapeDtypeStruct((BLOCK, depth), jnp.bfloat16 if other_rows else jnp.float32),
        scratch_shapes=[pltpu.VMEM((4, BLOCK, TILE), jnp.bfloat16)],
        compiler_params=params(24),
        cost_estimate=cost(2 * 8 * BLOCK * BLOCK * depth, 9 * BLOCK * depth * 2 + 8 * BLOCK * TILE * 2),
        name="apply_other" if other_rows else "apply_own",
    )(where, *mixing, *blocks)


def add(left, right):
    return (left.astype(jnp.float32) + right.astype(jnp.float32)).astype(jnp.bfloat16)


def gather_rings(sides):
    out = []
    for value, ring, pair in sides:
        first, there = lax.optimization_barrier([send(value, ring + "_first"), send(value, pair)])
        second, there_first = lax.optimization_barrier(
            [
                send(jnp.concatenate([value, first], axis=0), ring + "_second"),
                send(there, ring + "_first"),
            ]
        )
        there_second = send(jnp.concatenate([there, there_first], axis=0), ring + "_second")
        out.append([value, first, second, there, there_first, there_second])
    return out


def gather_even(value, ring, pair):
    there, first = send(value, pair), send(value, ring + "_first")
    second = send(jnp.concatenate([value, first], axis=0), ring + "_second")
    there_first = send(first, pair)
    there_second = send(jnp.concatenate([there, there_first], axis=0), ring + "_second")
    return [value, first, second, there, there_first, there_second]


def sum_over_col(tiles):
    own, first, second, there, there_first, there_second = tiles
    count = own.shape[0]
    there_pair = send(there_second, "z_second")
    pair = send(second, "z_second")
    there_from = send(add(there_first, there_pair[count:]), "z_first")
    first_from = send(add(first, pair[count:]), "z_first")
    there_sum = there.astype(jnp.float32) + there_pair[:count].astype(jnp.float32)
    there_sum = (there_sum + there_from.astype(jnp.float32)).astype(jnp.bfloat16)
    total = own.astype(jnp.float32) + pair[:count].astype(jnp.float32)
    total = total + first_from.astype(jnp.float32)
    total = total + send(there_sum, "yl").astype(jnp.float32)
    return total.astype(jnp.bfloat16)


def on_device(iterate):
    total_cols = iterate.shape[1] * lax.axis_size("col")
    row, col = lax.axis_index("row"), lax.axis_index("col")
    where = jnp.stack([row >> 2, (row >> 1) & 1, row & 1, col >> 2, col & 3]).astype(jnp.int32)
    iterate, where = lax.optimization_barrier((iterate, where))

    other, across, back, fore = lax.optimization_barrier(
        [send(iterate, move) for move in ("core", "yh", "x_back", "x_fore")]
    )
    across_other = send(across, "core")
    far = send(fore, "x_fore")
    rows = (iterate, other, across, across_other)
    near = gram_near(*rows, fore, back)
    gram_left = sum_over_col(gram_far(where, *rows, far, near))

    gram = jnp.concatenate([gram_left[:BLOCK], send(gram_left[BLOCK:], "core")], axis=1)
    left, right = gather_rings([(gram_left, "z", "yh"), (gram, "x", "yl")])
    mine, theirs = square_part(where, left, right)
    square = mine + send(theirs, "core").astype(jnp.float32)
    mixing = (cubic_coef * gram.astype(jnp.float32) + quintic_coef * square).astype(jnp.bfloat16)

    pieces = gather_even(mixing, "z", "yl")
    fore_other, back_other, far_other = (send(v, "core") for v in (back, fore, far))
    blocks = [iterate, other, fore, fore_other, back, back_other, far, far_other]
    applied_other = apply_part(True, where, pieces, blocks)
    applied = apply_part(False, where, pieces, blocks)
    update = applied + send(applied_other, "yh").astype(jnp.float32)
    return (math.sqrt(total_cols) * update).astype(jnp.bfloat16)


def solution(mesh):
    return jax.shard_map(
        on_device,
        mesh=mesh,
        in_specs=(P("row", "col"),),
        out_specs=P("row", "col"),
        check_vma=False,
    )
```

```python
import functools
import math

import jax
import jax.numpy as jnp
from jax import lax
from jax.experimental import pallas as pl
from jax.experimental.pallas import tpu as pltpu
from jax.sharding import PartitionSpec as P

linear_coef = 3.4445
cubic_coef = -4.775
quintic_coef = 2.0315

NX, NY, NC, NZ = 4, 2, 2, 4
BLOCK = 256
TILE = 2 * BLOCK
STRIP = 384
MIB = 1 << 20


def pairs(move):
    out = []
    for x in range(NX):
        for yh in range(NY):
            for core in range(NC):
                for yl in range(NY):
                    for z in range(NZ):
                        source = ((x * 2 + yh) * 2 + core) * 8 + yl * 4 + z
                        a, b, c, d, e = move(x, yh, core, yl, z)
                        a, e = a % NX, e % NZ
                        out.append((source, ((a * 2 + b) * 2 + c) * 8 + d * 4 + e))
    return out


def way(core):
    return 1 - 2 * core


MOVES = {
    "core": lambda x, yh, c, yl, z: (x, yh, 1 - c, yl, z),
    "yh": lambda x, yh, c, yl, z: (x, 1 - yh, c, yl, z),
    "yl": lambda x, yh, c, yl, z: (x, yh, c, 1 - yl, z),
    "x_fore": lambda x, yh, c, yl, z: (x + way(c), yh, c, yl, z),
    "x_back": lambda x, yh, c, yl, z: (x - way(c), yh, c, yl, z),
    "z_fore": lambda x, yh, c, yl, z: (x, yh, c, yl, z + way(c)),
    "z_back": lambda x, yh, c, yl, z: (x, yh, c, yl, z - way(c)),
}


def send(value, move):
    return lax.ppermute(value, ("row", "col"), pairs(MOVES[move]))


def place(delta, core):
    delta = lax.rem(delta + 8, 4)
    side = jnp.where(delta == 3 - 2 * core, 1, 2)
    return jnp.where(delta == 0, 0, jnp.where(delta == 2, 3, side))


def ahead(position, core):
    return (0, 2 * core - 1, 1 - 2 * core, 2)[position]


def nt(left, right):
    return lax.dot_general(left, right, (((1,), (1,)), ((), ())), preferred_element_type=jnp.float32)


def nn(left, right):
    return lax.dot_general(left, right, (((1,), (0,)), ((), ())), preferred_element_type=jnp.float32)


def gram_near_kernel(own, other, across, across_other, fore, out):
    for r, rows in enumerate((own, other, across, across_other)):
        for q, cols in enumerate((own, fore)):
            part = nt(rows[...], cols[...])
            out[r // 2, q, (r % 2) * BLOCK : (r % 2 + 1) * BLOCK] = part.astype(out.dtype)


def gram_far_kernel(where, own, other, across, across_other, back, far, near, *rest):
    outs, tiles = rest[:8], rest[8]
    x, yh, core, yl, z = (where[i] for i in range(5))
    for r, rows in enumerate((own, other, across, across_other)):
        for q, cols in enumerate((back, far)):
            part = nt(rows[...], cols[...])
            tiles[r // 2, q, (r % 2) * BLOCK : (r % 2 + 1) * BLOCK] = part.astype(tiles.dtype)
    for index, out in enumerate(outs):
        row = lax.rem(yl + index // 4 + yh, 2)
        col = place(z + ahead(index % 4, core) - x, core)

        @pl.when(col >= 2)
        def _():
            out[...] = tiles[row, jnp.maximum(col - 2, 0)]

        @pl.when(col < 2)
        def _():
            out[...] = near[row, jnp.minimum(col, 1)]


def square_kernel(where, *rest):
    left, right, (mine, theirs), (held,) = rest[:8], rest[8:16], rest[16:18], rest[18:]
    x, yh, core, yl, z = (where[i] for i in range(5))
    for dy in range(2):
        for position in range(4):
            held[dy, position] = right[dy * 4 + position][...]
    total = jnp.zeros((TILE, TILE), jnp.float32)
    for dy in range(2):
        for position in range(4):
            row = lax.rem(yh + dy + yl, 2)
            col = place(z + ahead(position, core) - x, core)
            total += nn(left[dy * 4 + position][...], held[row, col])
    mine[...] = total[:BLOCK]
    theirs[:, :BLOCK] = total[BLOCK:, BLOCK:].astype(theirs.dtype)
    theirs[:, BLOCK:] = total[BLOCK:, :BLOCK].astype(theirs.dtype)


def apply_kernel(other_rows, begin, where, *rest):
    mixing, blocks, (out, held) = rest[:8], rest[8:16], rest[16:]
    x, yh, core, yl, z = (where[i] for i in range(5))
    which = lax.rem(yh + yl + int(other_rows), 2)
    for dy in range(2):

        @pl.when(which == dy)
        def _():
            for position in range(4):
                col = place(z + ahead(position, core) - x, core)
                held[col] = mixing[dy * 4 + position][...]

    for start in range(0, out.shape[1], STRIP):
        columns = slice(begin + start, begin + start + STRIP)
        total = jnp.zeros((BLOCK, STRIP), jnp.float32)
        for position in range(4):
            for half in range(2):
                total += nn(
                    held[position, :, half * BLOCK : (half + 1) * BLOCK],
                    blocks[position * 2 + half][:, columns],
                )
        if not other_rows:
            total = total + linear_coef * blocks[0][:, columns].astype(jnp.float32)
        out[:, start : start + STRIP] = total.astype(out.dtype)


def params(mib):
    return pltpu.CompilerParams(vmem_limit_bytes=mib * MIB)


def smem():
    return pl.BlockSpec(memory_space=pltpu.SMEM)


def whole():
    return pl.BlockSpec(memory_space=pltpu.VMEM)


def cost(flops, moved):
    return pl.CostEstimate(flops=flops, bytes_accessed=moved, transcendentals=0)


def gram_near(own, other, across, across_other, fore):
    depth = own.shape[1]
    return pl.pallas_call(
        gram_near_kernel,
        in_specs=[whole() for _ in range(5)],
        out_specs=whole(),
        out_shape=jax.ShapeDtypeStruct((2, 2, TILE, BLOCK), jnp.bfloat16),
        compiler_params=params(24),
        cost_estimate=cost(2 * 4 * BLOCK * TILE * depth, 5 * BLOCK * depth * 2 + 4 * BLOCK * TILE * 2),
        name="gram_near",
    )(own, other, across, across_other, fore)


def gram_far(where, own, other, across, across_other, back, far, near):
    depth = own.shape[1]
    return pl.pallas_call(
        gram_far_kernel,
        in_specs=[smem()] + [whole() for _ in range(7)],
        out_specs=[whole() for _ in range(8)],
        out_shape=[jax.ShapeDtypeStruct((TILE, BLOCK), jnp.bfloat16) for _ in range(8)],
        scratch_shapes=[pltpu.VMEM((2, 2, TILE, BLOCK), jnp.bfloat16)],
        compiler_params=params(24),
        cost_estimate=cost(2 * 4 * BLOCK * TILE * depth, 6 * BLOCK * depth * 2 + 12 * BLOCK * TILE * 2),
        name="gram_far",
    )(where, own, other, across, across_other, back, far, near)


def square_part(where, left, right):
    return pl.pallas_call(
        square_kernel,
        in_specs=[smem()] + [whole() for _ in range(16)],
        out_specs=[whole(), whole()],
        out_shape=[
            jax.ShapeDtypeStruct((BLOCK, TILE), jnp.float32),
            jax.ShapeDtypeStruct((BLOCK, TILE), jnp.bfloat16),
        ],
        scratch_shapes=[pltpu.VMEM((2, 4, BLOCK, TILE), jnp.bfloat16)],
        compiler_params=params(24),
        cost_estimate=cost(2 * 8 * TILE * TILE * BLOCK, 16 * BLOCK * TILE * 2),
        name="square_part",
    )(where, *left, *right)


def apply_part(other_rows, begin, width, where, mixing, blocks):
    return pl.pallas_call(
        functools.partial(apply_kernel, other_rows, begin),
        in_specs=[smem()] + [whole() for _ in range(16)],
        out_specs=whole(),
        out_shape=jax.ShapeDtypeStruct((BLOCK, width), jnp.bfloat16 if other_rows else jnp.float32),
        scratch_shapes=[pltpu.VMEM((4, BLOCK, TILE), jnp.bfloat16)],
        compiler_params=params(24),
        cost_estimate=cost(2 * 8 * BLOCK * BLOCK * width, 9 * BLOCK * width * 2 + 8 * BLOCK * TILE * 2),
        name="apply_other" if other_rows else "apply_own",
    )(where, *mixing, *blocks)


def add(left, right):
    return (left.astype(jnp.float32) + right.astype(jnp.float32)).astype(jnp.bfloat16)


def gather_rings(sides):
    first = [
        [send(value, ring + "_back"), send(value, ring + "_fore"), send(value, pair)]
        for value, ring, pair in sides
    ]
    first = [lax.optimization_barrier(part) for part in first]
    second = [
        [
            send(there, ring + "_back"),
            send(jnp.concatenate([there, fore], axis=0), ring + "_fore"),
        ]
        for (back, fore, there), (value, ring, pair) in zip(first, sides)
    ]
    second = [lax.optimization_barrier(part) for part in second]
    out = []
    for (back, fore, there), (there_back, both), (value, ring, pair) in zip(first, second, sides):
        count = value.shape[0]
        there_fore, far = both[:count], both[count:]
        there_far = send(there_fore, ring + "_fore")
        out.append([value, fore, back, far, there, there_fore, there_back, there_far])
    return out


def gather_even(value, ring, pair):
    fore, back = send(value, ring + "_fore"), send(value, ring + "_back")
    there = send(value, pair)
    far = send(fore, ring + "_fore")
    there_fore = send(there, ring + "_fore")
    there_back = send(back, pair)
    there_far = send(there_fore, ring + "_fore")
    return [value, fore, back, far, there, there_fore, there_back, there_far]


def sum_over_col(tiles):
    chain = add(tiles[5], send(tiles[7], "z_back"))
    back = add(tiles[1], send(tiles[3], "z_back"))
    fore = add(tiles[2], send(tiles[6], "yl"))
    there = add(tiles[4], send(chain, "z_back"))
    total = tiles[0].astype(jnp.float32)
    total = total + send(back, "z_back").astype(jnp.float32)
    total = total + send(fore, "z_fore").astype(jnp.float32)
    total = total + send(there, "yl").astype(jnp.float32)
    return total.astype(jnp.bfloat16)


def on_device(iterate):
    total_cols = iterate.shape[1] * lax.axis_size("col")
    row, col = lax.axis_index("row"), lax.axis_index("col")
    where = jnp.stack([row >> 2, (row >> 1) & 1, row & 1, col >> 2, col & 3]).astype(jnp.int32)
    iterate, where = lax.optimization_barrier((iterate, where))

    half = BLOCK // 2
    other, across_top, fore, iterate = lax.optimization_barrier(
        [send(iterate, "core"), send(iterate[:half], "yh"), send(iterate, "x_fore"), iterate]
    )
    across_low, back, far = lax.optimization_barrier(
        [send(iterate[half:], "yh"), send(iterate, "x_back"), send(fore, "x_fore")]
    )
    across = jnp.concatenate([across_top, across_low], axis=0)
    rows = (iterate, other, across, send(across, "core"))
    near = gram_near(*rows, fore)
    gram_left = sum_over_col(gram_far(where, *rows, back, far, near))

    gram = jnp.concatenate([gram_left[:BLOCK], send(gram_left[BLOCK:], "core")], axis=1)
    left, right = gather_rings([(gram_left, "z", "yh"), (gram, "x", "yl")])
    mine, theirs = square_part(where, left, right)
    square = mine + send(theirs, "core").astype(jnp.float32)
    mixing = (cubic_coef * gram.astype(jnp.float32) + quintic_coef * square).astype(jnp.bfloat16)

    pieces = gather_even(mixing, "z", "yl")
    fore_other, back_other, far_other = (send(v, "core") for v in (back, fore, far))
    blocks = [iterate, other, fore, fore_other, back, back_other, far, far_other]
    depth = iterate.shape[1]
    swapped = []
    for begin in (0, depth // 2):
        swapped.append(send(apply_part(True, begin, depth // 2, where, pieces, blocks), "yh"))
    applied = apply_part(False, 0, depth, where, pieces, blocks)
    update = applied + jnp.concatenate(swapped, axis=1).astype(jnp.float32)
    return (math.sqrt(total_cols) * update).astype(jnp.bfloat16)


def solution(mesh):
    return jax.shard_map(
        on_device,
        mesh=mesh,
        in_specs=(P("row", "col"),),
        out_specs=P("row", "col"),
        check_vma=False,
    )
```

```python
import functools
import math

import jax
import jax.numpy as jnp
from jax import lax
from jax.experimental import pallas as pl
from jax.experimental.pallas import tpu as pltpu
from jax.sharding import PartitionSpec as P

linear_coef = 3.4445
cubic_coef = -4.775
quintic_coef = 2.0315

NX, NY, NC, NZ = 4, 2, 2, 4
BLOCK = 256
TILE = 2 * BLOCK
STRIP = 384
MIB = 1 << 20


def pairs(move):
    out = []
    for x in range(NX):
        for yh in range(NY):
            for core in range(NC):
                for yl in range(NY):
                    for z in range(NZ):
                        source = ((x * 2 + yh) * 2 + core) * 8 + yl * 4 + z
                        a, b, c, d, e = move(x, yh, core, yl, z)
                        a, e = a % NX, e % NZ
                        out.append((source, ((a * 2 + b) * 2 + c) * 8 + d * 4 + e))
    return out


def way(core):
    return 1 - 2 * core


MOVES = {
    "core": lambda x, yh, c, yl, z: (x, yh, 1 - c, yl, z),
    "yh": lambda x, yh, c, yl, z: (x, 1 - yh, c, yl, z),
    "yl": lambda x, yh, c, yl, z: (x, yh, c, 1 - yl, z),
    "x_fore": lambda x, yh, c, yl, z: (x + way(c), yh, c, yl, z),
    "x_back": lambda x, yh, c, yl, z: (x - way(c), yh, c, yl, z),
    "z_fore": lambda x, yh, c, yl, z: (x, yh, c, yl, z + way(c)),
    "z_back": lambda x, yh, c, yl, z: (x, yh, c, yl, z - way(c)),
}


def send(value, move):
    return lax.ppermute(value, ("row", "col"), pairs(MOVES[move]))


def place(delta, core):
    delta = lax.rem(delta + 8, 4)
    side = jnp.where(delta == 3 - 2 * core, 1, 2)
    return jnp.where(delta == 0, 0, jnp.where(delta == 2, 3, side))


def ahead(position, core):
    return (0, 2 * core - 1, 1 - 2 * core, 2)[position]


def nt(left, right):
    return lax.dot_general(left, right, (((1,), (1,)), ((), ())), preferred_element_type=jnp.float32)


def nn(left, right):
    return lax.dot_general(left, right, (((1,), (0,)), ((), ())), preferred_element_type=jnp.float32)


def gram_kernel(where, own, other, across, across_other, fore, back, far, *rest):
    outs, tiles = rest[:8], rest[8]
    x, yh, core, yl, z = (where[i] for i in range(5))
    for r, rows in enumerate((own, other, across, across_other)):
        for q, cols in enumerate((own, fore, back, far)):
            part = nt(rows[...], cols[...])
            tiles[r // 2, q, (r % 2) * BLOCK : (r % 2 + 1) * BLOCK] = part.astype(tiles.dtype)
    for index, out in enumerate(outs):
        row = lax.rem(yl + index // 4 + yh, 2)
        col = place(z + ahead(index % 4, core) - x, core)
        out[...] = tiles[row, col]


def square_kernel(where, *rest):
    left, right, (mine, theirs), (held,) = rest[:8], rest[8:16], rest[16:18], rest[18:]
    x, yh, core, yl, z = (where[i] for i in range(5))
    for dy in range(2):
        for position in range(4):
            held[dy, position] = right[dy * 4 + position][...]
    total = jnp.zeros((TILE, TILE), jnp.float32)
    for dy in range(2):
        for position in range(4):
            row = lax.rem(yh + dy + yl, 2)
            col = place(z + ahead(position, core) - x, core)
            total += nn(left[dy * 4 + position][...], held[row, col])
    mine[...] = total[:BLOCK]
    theirs[:, :BLOCK] = total[BLOCK:, BLOCK:].astype(theirs.dtype)
    theirs[:, BLOCK:] = total[BLOCK:, :BLOCK].astype(theirs.dtype)


def apply_kernel(other_rows, begin, where, *rest):
    mixing, blocks, (out, held) = rest[:8], rest[8:16], rest[16:]
    x, yh, core, yl, z = (where[i] for i in range(5))
    which = lax.rem(yh + yl + int(other_rows), 2)
    for dy in range(2):

        @pl.when(which == dy)
        def _():
            for position in range(4):
                col = place(z + ahead(position, core) - x, core)
                held[col] = mixing[dy * 4 + position][...]

    for start in range(0, out.shape[1], STRIP):
        columns = slice(begin + start, begin + start + STRIP)
        total = jnp.zeros((BLOCK, STRIP), jnp.float32)
        for position in range(4):
            for half in range(2):
                total += nn(
                    held[position, :, half * BLOCK : (half + 1) * BLOCK],
                    blocks[position * 2 + half][:, columns],
                )
        if not other_rows:
            total = total + linear_coef * blocks[0][:, columns].astype(jnp.float32)
        out[:, start : start + STRIP] = total.astype(out.dtype)


def params(mib):
    return pltpu.CompilerParams(vmem_limit_bytes=mib * MIB)


def smem():
    return pl.BlockSpec(memory_space=pltpu.SMEM)


def whole():
    return pl.BlockSpec(memory_space=pltpu.VMEM)


def cost(flops, moved):
    return pl.CostEstimate(flops=flops, bytes_accessed=moved, transcendentals=0)


def gram_tiles(where, own, other, across, across_other, fore, back, far):
    depth = own.shape[1]
    return pl.pallas_call(
        gram_kernel,
        in_specs=[smem()] + [whole() for _ in range(7)],
        out_specs=[whole() for _ in range(8)],
        out_shape=[jax.ShapeDtypeStruct((TILE, BLOCK), jnp.bfloat16) for _ in range(8)],
        scratch_shapes=[pltpu.VMEM((2, 4, TILE, BLOCK), jnp.bfloat16)],
        compiler_params=params(24),
        cost_estimate=cost(2 * 8 * BLOCK * TILE * depth, 7 * BLOCK * depth * 2 + 8 * BLOCK * TILE * 2),
        name="gram_tiles",
    )(where, own, other, across, across_other, fore, back, far)


def square_part(where, left, right):
    return pl.pallas_call(
        square_kernel,
        in_specs=[smem()] + [whole() for _ in range(16)],
        out_specs=[whole(), whole()],
        out_shape=[
            jax.ShapeDtypeStruct((BLOCK, TILE), jnp.float32),
            jax.ShapeDtypeStruct((BLOCK, TILE), jnp.bfloat16),
        ],
        scratch_shapes=[pltpu.VMEM((2, 4, BLOCK, TILE), jnp.bfloat16)],
        compiler_params=params(24),
        cost_estimate=cost(2 * 8 * TILE * TILE * BLOCK, 16 * BLOCK * TILE * 2),
        name="square_part",
    )(where, *left, *right)


def apply_part(other_rows, begin, width, where, mixing, blocks):
    return pl.pallas_call(
        functools.partial(apply_kernel, other_rows, begin),
        in_specs=[smem()] + [whole() for _ in range(16)],
        out_specs=whole(),
        out_shape=jax.ShapeDtypeStruct((BLOCK, width), jnp.bfloat16 if other_rows else jnp.float32),
        scratch_shapes=[pltpu.VMEM((4, BLOCK, TILE), jnp.bfloat16)],
        compiler_params=params(24),
        cost_estimate=cost(2 * 8 * BLOCK * BLOCK * width, 9 * BLOCK * width * 2 + 8 * BLOCK * TILE * 2),
        name="apply_other" if other_rows else "apply_own",
    )(where, *mixing, *blocks)


def add(left, right):
    return (left.astype(jnp.float32) + right.astype(jnp.float32)).astype(jnp.bfloat16)


def gather_even(value, ring, pair):
    fore, back = send(value, ring + "_fore"), send(value, ring + "_back")
    there = send(value, pair)
    far = send(fore, ring + "_fore")
    there_fore = send(there, ring + "_fore")
    there_back = send(back, pair)
    there_far = send(there_fore, ring + "_fore")
    return [value, fore, back, far, there, there_fore, there_back, there_far]


def sum_over_col(tiles):
    chain = add(tiles[5], send(tiles[7], "z_back"))
    back = add(tiles[1], send(tiles[3], "z_back"))
    fore = add(tiles[2], send(tiles[6], "yl"))
    there = add(tiles[4], send(chain, "z_back"))
    total = tiles[0].astype(jnp.float32)
    total = total + send(back, "z_back").astype(jnp.float32)
    total = total + send(fore, "z_fore").astype(jnp.float32)
    total = total + send(there, "yl").astype(jnp.float32)
    return total.astype(jnp.bfloat16)


def on_device(iterate):
    total_cols = iterate.shape[1] * lax.axis_size("col")
    row, col = lax.axis_index("row"), lax.axis_index("col")
    where = jnp.stack([row >> 2, (row >> 1) & 1, row & 1, col >> 2, col & 3]).astype(jnp.int32)
    iterate, where = lax.optimization_barrier((iterate, where))

    half = BLOCK // 2
    across = send(iterate, "yh")
    other, back, low = lax.optimization_barrier(
        [send(iterate, "core"), send(iterate, "x_back"), send(iterate[half:], "x_fore")]
    )
    top = send(iterate[:half], "x_fore")
    far = [send(top, "x_fore"), send(low, "x_fore")]
    fore = jnp.concatenate([top, low], axis=0)
    far = jnp.concatenate(far, axis=0)
    rows = (iterate, other, across, send(across, "core"))
    gram_left = sum_over_col(gram_tiles(where, *rows, fore, back, far))

    gram = jnp.concatenate([gram_left[:BLOCK], send(gram_left[BLOCK:], "core")], axis=1)
    left, right = gather_even(gram_left, "z", "yh"), gather_even(gram, "x", "yl")
    mine, theirs = square_part(where, left, right)
    square = mine + send(theirs, "core").astype(jnp.float32)
    mixing = (cubic_coef * gram.astype(jnp.float32) + quintic_coef * square).astype(jnp.bfloat16)

    pieces = gather_even(mixing, "z", "yl")
    fore_other, back_other, far_other = (send(v, "core") for v in (back, fore, far))
    blocks = [iterate, other, fore, fore_other, back, back_other, far, far_other]
    depth = iterate.shape[1]
    swapped = []
    for begin in (0, depth // 2):
        swapped.append(send(apply_part(True, begin, depth // 2, where, pieces, blocks), "yh"))
    applied = apply_part(False, 0, depth, where, pieces, blocks)
    update = applied + jnp.concatenate(swapped, axis=1).astype(jnp.float32)
    return (math.sqrt(total_cols) * update).astype(jnp.bfloat16)


def solution(mesh):
    return jax.shard_map(
        on_device,
        mesh=mesh,
        in_specs=(P("row", "col"),),
        out_specs=P("row", "col"),
        check_vma=False,
    )
```

```python
import functools
import math

import jax
import jax.numpy as jnp
from jax import lax
from jax.experimental import pallas as pl
from jax.experimental.pallas import tpu as pltpu
from jax.sharding import PartitionSpec as P

linear_coef = 3.4445
cubic_coef = -4.775
quintic_coef = 2.0315

NX, NY, NC, NZ = 4, 2, 2, 4
BLOCK = 256
TILE = 2 * BLOCK
STRIP = 384
MIB = 1 << 20


def pairs(move):
    out = []
    for x in range(NX):
        for yh in range(NY):
            for core in range(NC):
                for yl in range(NY):
                    for z in range(NZ):
                        source = ((x * 2 + yh) * 2 + core) * 8 + yl * 4 + z
                        a, b, c, d, e = move(x, yh, core, yl, z)
                        a, e = a % NX, e % NZ
                        out.append((source, ((a * 2 + b) * 2 + c) * 8 + d * 4 + e))
    return out


def way(core):
    return 1 - 2 * core


MOVES = {
    "core": lambda x, yh, c, yl, z: (x, yh, 1 - c, yl, z),
    "yh": lambda x, yh, c, yl, z: (x, 1 - yh, c, yl, z),
    "yl": lambda x, yh, c, yl, z: (x, yh, c, 1 - yl, z),
    "turn": lambda x, yh, c, yl, z: (x, yl, c, yh, z),
    "turn_yl": lambda x, yh, c, yl, z: (x, yl, c, 1 - yh, z),
    "x_fore": lambda x, yh, c, yl, z: (x + way(c), yh, c, yl, z),
    "x_back": lambda x, yh, c, yl, z: (x - way(c), yh, c, yl, z),
    "z_fore": lambda x, yh, c, yl, z: (x, yh, c, yl, z + way(c)),
    "z_back": lambda x, yh, c, yl, z: (x, yh, c, yl, z - way(c)),
}


def send(value, move):
    return lax.ppermute(value, ("row", "col"), pairs(MOVES[move]))


def place(delta, core):
    delta = lax.rem(delta + 8, 4)
    side = jnp.where(delta == 3 - 2 * core, 1, 2)
    return jnp.where(delta == 0, 0, jnp.where(delta == 2, 3, side))


def ahead(position, core):
    return (0, 2 * core - 1, 1 - 2 * core, 2)[position]


def nt(left, right):
    return lax.dot_general(left, right, (((1,), (1,)), ((), ())), preferred_element_type=jnp.float32)


def nn(left, right):
    return lax.dot_general(left, right, (((1,), (0,)), ((), ())), preferred_element_type=jnp.float32)


def gram_kernel(where, own, other, across, across_other, fore, back, far, *rest):
    outs, tiles = rest[:8], rest[8]
    x, yh, core, yl, z = (where[i] for i in range(5))
    for r, rows in enumerate((own, other, across, across_other)):
        for q, cols in enumerate((own, fore, back, far)):
            part = nt(rows[...], cols[...])
            tiles[r // 2, q, (r % 2) * BLOCK : (r % 2 + 1) * BLOCK] = part.astype(tiles.dtype)
    for index, out in enumerate(outs):
        row = lax.rem(yl + index // 4 + yh, 2)
        col = place(z + ahead(index % 4, core) - x, core)
        out[...] = tiles[row, col]


def square_kernel(where, *rest):
    left, right, (mine, theirs), (held,) = rest[:8], rest[8:16], rest[16:18], rest[18:]
    x, yh, core, yl, z = (where[i] for i in range(5))
    for dy in range(2):
        for position in range(4):
            held[dy, position] = right[dy * 4 + position][...]
    total = jnp.zeros((TILE, TILE), jnp.float32)
    for dy in range(2):
        for position in range(4):
            row = lax.rem(yh + dy + yl, 2)
            col = place(z + ahead(position, core) - x, core)
            total += nn(left[dy * 4 + position][...], held[row, col])
    mine[...] = total[:, :BLOCK]
    theirs[:BLOCK] = total[BLOCK:, BLOCK:].astype(theirs.dtype)
    theirs[BLOCK:] = total[:BLOCK, BLOCK:].astype(theirs.dtype)


def apply_kernel(other_rows, begin, where, *rest):
    mixing, blocks, (out, held) = rest[:8], rest[8:16], rest[16:]
    x, yh, core, yl, z = (where[i] for i in range(5))
    for index in range(8):
        row = lax.rem(yl + index // 4 + yh, 2)
        col = place(z + ahead(index % 4, core) - x, core)
        held[row, col] = mixing[index][int(other_rows) * BLOCK : (int(other_rows) + 1) * BLOCK]

    for start in range(0, out.shape[1], STRIP):
        columns = slice(begin + start, begin + start + STRIP)
        total = jnp.zeros((BLOCK, STRIP), jnp.float32)
        for index in range(8):
            total += nn(held[index // 4, index % 4], blocks[index][:, columns])
        if not other_rows:
            total = total + linear_coef * blocks[0][:, columns].astype(jnp.float32)
        out[:, start : start + STRIP] = total.astype(out.dtype)


def params(mib):
    return pltpu.CompilerParams(vmem_limit_bytes=mib * MIB)


def smem():
    return pl.BlockSpec(memory_space=pltpu.SMEM)


def whole():
    return pl.BlockSpec(memory_space=pltpu.VMEM)


def cost(flops, moved):
    return pl.CostEstimate(flops=flops, bytes_accessed=moved, transcendentals=0)


def gram_tiles(where, own, other, across, across_other, fore, back, far):
    depth = own.shape[1]
    return pl.pallas_call(
        gram_kernel,
        in_specs=[smem()] + [whole() for _ in range(7)],
        out_specs=[whole() for _ in range(8)],
        out_shape=[jax.ShapeDtypeStruct((TILE, BLOCK), jnp.bfloat16) for _ in range(8)],
        scratch_shapes=[pltpu.VMEM((2, 4, TILE, BLOCK), jnp.bfloat16)],
        compiler_params=params(24),
        cost_estimate=cost(2 * 8 * BLOCK * TILE * depth, 7 * BLOCK * depth * 2 + 8 * BLOCK * TILE * 2),
        name="gram_tiles",
    )(where, own, other, across, across_other, fore, back, far)


def square_part(where, left, right):
    return pl.pallas_call(
        square_kernel,
        in_specs=[smem()] + [whole() for _ in range(16)],
        out_specs=[whole(), whole()],
        out_shape=[
            jax.ShapeDtypeStruct((TILE, BLOCK), jnp.float32),
            jax.ShapeDtypeStruct((TILE, BLOCK), jnp.bfloat16),
        ],
        scratch_shapes=[pltpu.VMEM((2, 4, BLOCK, TILE), jnp.bfloat16)],
        compiler_params=params(24),
        cost_estimate=cost(2 * 8 * TILE * TILE * BLOCK, 16 * BLOCK * TILE * 2),
        name="square_part",
    )(where, *left, *right)


def apply_part(other_rows, begin, width, where, mixing, blocks):
    return pl.pallas_call(
        functools.partial(apply_kernel, other_rows, begin),
        in_specs=[smem()] + [whole() for _ in range(16)],
        out_specs=whole(),
        out_shape=jax.ShapeDtypeStruct((BLOCK, width), jnp.bfloat16 if other_rows else jnp.float32),
        scratch_shapes=[pltpu.VMEM((2, 4, BLOCK, BLOCK), jnp.bfloat16)],
        compiler_params=params(24),
        cost_estimate=cost(2 * 8 * BLOCK * BLOCK * width, 9 * BLOCK * width * 2 + 8 * BLOCK * TILE * 2),
        name="apply_other" if other_rows else "apply_own",
    )(where, *mixing, *blocks)


def add(left, right):
    return (left.astype(jnp.float32) + right.astype(jnp.float32)).astype(jnp.bfloat16)


def gather_even(value, ring, pair, there=None):
    fore, back = send(value, ring + "_fore"), send(value, ring + "_back")
    there = send(value, pair) if there is None else there
    far = send(fore, ring + "_fore")
    there_fore = send(there, ring + "_fore")
    there_back = send(back, pair)
    there_far = send(there_fore, ring + "_fore")
    return [value, fore, back, far, there, there_fore, there_back, there_far]


def sum_over_col(tiles):
    chain = add(tiles[5], send(tiles[7], "z_back"))
    back = add(tiles[1], send(tiles[3], "z_back"))
    fore = add(tiles[2], send(tiles[6], "yl"))
    there = add(tiles[4], send(chain, "z_back"))
    total = tiles[0].astype(jnp.float32)
    total = total + send(back, "z_back").astype(jnp.float32)
    total = total + send(fore, "z_fore").astype(jnp.float32)
    total = total + send(there, "yl").astype(jnp.float32)
    return total.astype(jnp.bfloat16)


def on_device(iterate):
    total_cols = iterate.shape[1] * lax.axis_size("col")
    row, col = lax.axis_index("row"), lax.axis_index("col")
    where = jnp.stack([row >> 2, (row >> 1) & 1, row & 1, col >> 2, col & 3]).astype(jnp.int32)
    iterate, where = lax.optimization_barrier((iterate, where))

    half = BLOCK // 2
    across = send(iterate, "yh")
    other, back, low = lax.optimization_barrier(
        [send(iterate, "core"), send(iterate, "x_back"), send(iterate[half:], "x_fore")]
    )
    top = send(iterate[:half], "x_fore")
    far = [send(top, "x_fore"), send(low, "x_fore")]
    fore = jnp.concatenate([top, low], axis=0)
    far = jnp.concatenate(far, axis=0)
    rows = (iterate, other, across, send(across, "core"))
    gram_left = sum_over_col(gram_tiles(where, *rows, fore, back, far))

    across_fore, across_back = send(across, "x_fore"), send(across, "x_back")
    gram_left, across_fore, across_back = lax.optimization_barrier((gram_left, across_fore, across_back))
    across_far = send(across_fore, "x_fore")
    gram = jnp.concatenate([gram_left[:BLOCK], send(gram_left[BLOCK:], "core")], axis=1)
    left, right = gather_even(gram_left, "z", "yh"), gather_even(gram, "x", "yl")
    mine, theirs = square_part(where, left, right)
    square = mine + send(theirs, "core").astype(jnp.float32)
    mixing = (cubic_coef * gram_left.astype(jnp.float32) + quintic_coef * square).astype(jnp.bfloat16)

    there = send(mixing, "turn_yl")
    pieces = gather_even(send(mixing, "turn"), "z", "yl", there)
    blocks = [iterate, fore, back, far, across, across_fore, across_back, across_far]
    depth = iterate.shape[1]
    swapped = []
    for begin in (0, depth // 2):
        swapped.append(send(apply_part(True, begin, depth // 2, where, pieces, blocks), "core"))
    applied = apply_part(False, 0, depth, where, pieces, blocks)
    update = applied + jnp.concatenate(swapped, axis=1).astype(jnp.float32)
    return (math.sqrt(total_cols) * update).astype(jnp.bfloat16)


def solution(mesh):
    return jax.shard_map(
        on_device,
        mesh=mesh,
        in_specs=(P("row", "col"),),
        out_specs=P("row", "col"),
        check_vma=False,
    )
```

```python
import functools
import math

import jax
import jax.numpy as jnp
from jax import lax
from jax.experimental import pallas as pl
from jax.experimental.pallas import tpu as pltpu
from jax.sharding import PartitionSpec as P

linear_coef = 3.4445
cubic_coef = -4.775
quintic_coef = 2.0315

NX, NY, NC, NZ = 4, 2, 2, 4
BLOCK = 256
TILE = 2 * BLOCK
STRIP = 768
MIB = 1 << 20


def pairs(move):
    out = []
    for x in range(NX):
        for yh in range(NY):
            for core in range(NC):
                for yl in range(NY):
                    for z in range(NZ):
                        source = ((x * 2 + yh) * 2 + core) * 8 + yl * 4 + z
                        a, b, c, d, e = move(x, yh, core, yl, z)
                        a, e = a % NX, e % NZ
                        out.append((source, ((a * 2 + b) * 2 + c) * 8 + d * 4 + e))
    return out


def way(core):
    return 1 - 2 * core


MOVES = {
    "core": lambda x, yh, c, yl, z: (x, yh, 1 - c, yl, z),
    "yh": lambda x, yh, c, yl, z: (x, 1 - yh, c, yl, z),
    "yl": lambda x, yh, c, yl, z: (x, yh, c, 1 - yl, z),
    "turn": lambda x, yh, c, yl, z: (x, yl, c, yh, z),
    "turn_yl": lambda x, yh, c, yl, z: (x, yl, c, 1 - yh, z),
    "x_fore": lambda x, yh, c, yl, z: (x + way(c), yh, c, yl, z),
    "x_back": lambda x, yh, c, yl, z: (x - way(c), yh, c, yl, z),
    "z_fore": lambda x, yh, c, yl, z: (x, yh, c, yl, z + way(c)),
    "z_back": lambda x, yh, c, yl, z: (x, yh, c, yl, z - way(c)),
}


def send(value, move):
    return lax.ppermute(value, ("row", "col"), pairs(MOVES[move]))


def place(delta, core):
    delta = lax.rem(delta + 8, 4)
    side = jnp.where(delta == 3 - 2 * core, 1, 2)
    return jnp.where(delta == 0, 0, jnp.where(delta == 2, 3, side))


def ahead(position, core):
    return (0, 2 * core - 1, 1 - 2 * core, 2)[position]


def nt(left, right):
    return lax.dot_general(left, right, (((1,), (1,)), ((), ())), preferred_element_type=jnp.float32)


def nn(left, right):
    return lax.dot_general(left, right, (((1,), (0,)), ((), ())), preferred_element_type=jnp.float32)


def gram_near_kernel(own, other, fore, back, out):
    for r, rows in enumerate((own, other)):
        for q, cols in enumerate((own, fore, back)):
            part = nt(rows[...], cols[...])
            out[q, r * BLOCK : (r + 1) * BLOCK] = part.astype(out.dtype)


def gram_kernel(where, own, other, across, across_other, fore, back, far, near, *rest):
    outs, tiles = rest[:8], rest[8]
    x, yh, core, yl, z = (where[i] for i in range(5))
    tiles[0, :3] = near[...]
    for r, rows in enumerate((own, other)):
        part = nt(rows[...], far[...])
        tiles[0, 3, r * BLOCK : (r + 1) * BLOCK] = part.astype(tiles.dtype)
    for r, rows in enumerate((across, across_other)):
        for q, cols in enumerate((own, fore, back, far)):
            part = nt(rows[...], cols[...])
            tiles[1, q, r * BLOCK : (r + 1) * BLOCK] = part.astype(tiles.dtype)
    for index, out in enumerate(outs):
        row = lax.rem(yl + index // 4 + yh, 2)
        col = place(z + ahead(index % 4, core) - x, core)
        out[...] = tiles[row, col]


def square_kernel(where, *rest):
    left, right, (mine, theirs), (held,) = rest[:8], rest[8:16], rest[16:18], rest[18:]
    x, yh, core, yl, z = (where[i] for i in range(5))
    for dy in range(2):
        for position in range(4):
            held[dy, position] = right[dy * 4 + position][...]
    total = jnp.zeros((TILE, TILE), jnp.float32)
    for dy in range(2):
        for position in range(4):
            row = lax.rem(yh + dy + yl, 2)
            col = place(z + ahead(position, core) - x, core)
            total += nn(left[dy * 4 + position][...], held[row, col])
    mine[...] = total[:, :BLOCK]
    theirs[:BLOCK] = total[BLOCK:, BLOCK:].astype(theirs.dtype)
    theirs[BLOCK:] = total[:BLOCK, BLOCK:].astype(theirs.dtype)


def apply_kernel(begin, where, *rest):
    mixing, blocks, (mine, theirs, held) = rest[:8], rest[8:16], rest[16:]
    x, yh, core, yl, z = (where[i] for i in range(5))
    for index in range(8):
        row = lax.rem(yl + index // 4 + yh, 2)
        col = place(z + ahead(index % 4, core) - x, core)
        lanes = pl.ds(pl.multiple_of((row * 4 + col) * BLOCK, BLOCK), BLOCK)
        held[:, lanes] = mixing[index][...]

    for start in range(0, mine.shape[1], STRIP):
        columns = slice(begin + start, begin + start + STRIP)
        total = nn(held[...], jnp.concatenate([block[:, columns] for block in blocks], axis=0))
        theirs[:, start : start + STRIP] = total[BLOCK:].astype(theirs.dtype)
        total = total[:BLOCK] + linear_coef * blocks[0][:, columns].astype(jnp.float32)
        mine[:, start : start + STRIP] = total


def params(mib):
    return pltpu.CompilerParams(vmem_limit_bytes=mib * MIB)


def smem():
    return pl.BlockSpec(memory_space=pltpu.SMEM)


def whole():
    return pl.BlockSpec(memory_space=pltpu.VMEM)


def cost(flops, moved):
    return pl.CostEstimate(flops=flops, bytes_accessed=moved, transcendentals=0)


def gram_near(own, other, fore, back):
    depth = own.shape[1]
    return pl.pallas_call(
        gram_near_kernel,
        in_specs=[whole() for _ in range(4)],
        out_specs=whole(),
        out_shape=jax.ShapeDtypeStruct((3, TILE, BLOCK), jnp.bfloat16),
        compiler_params=params(24),
        cost_estimate=cost(2 * 3 * BLOCK * TILE * depth, 4 * BLOCK * depth * 2 + 3 * BLOCK * TILE * 2),
        name="gram_near",
    )(own, other, fore, back)


def gram_tiles(where, own, other, across, across_other, fore, back, far, near):
    depth = own.shape[1]
    return pl.pallas_call(
        gram_kernel,
        in_specs=[smem()] + [whole() for _ in range(8)],
        out_specs=[whole() for _ in range(8)],
        out_shape=[jax.ShapeDtypeStruct((TILE, BLOCK), jnp.bfloat16) for _ in range(8)],
        scratch_shapes=[pltpu.VMEM((2, 4, TILE, BLOCK), jnp.bfloat16)],
        compiler_params=params(24),
        cost_estimate=cost(2 * 5 * BLOCK * TILE * depth, 7 * BLOCK * depth * 2 + 11 * BLOCK * TILE * 2),
        name="gram_tiles",
    )(where, own, other, across, across_other, fore, back, far, near)


def square_part(where, left, right):
    return pl.pallas_call(
        square_kernel,
        in_specs=[smem()] + [whole() for _ in range(16)],
        out_specs=[whole(), whole()],
        out_shape=[
            jax.ShapeDtypeStruct((TILE, BLOCK), jnp.float32),
            jax.ShapeDtypeStruct((TILE, BLOCK), jnp.bfloat16),
        ],
        scratch_shapes=[pltpu.VMEM((2, 4, BLOCK, TILE), jnp.bfloat16)],
        compiler_params=params(24),
        cost_estimate=cost(2 * 8 * TILE * TILE * BLOCK, 16 * BLOCK * TILE * 2),
        name="square_part",
    )(where, *left, *right)


def apply_part(begin, width, where, mixing, blocks):
    return pl.pallas_call(
        functools.partial(apply_kernel, begin),
        in_specs=[smem()] + [whole() for _ in range(16)],
        out_specs=[whole(), whole()],
        out_shape=[
            jax.ShapeDtypeStruct((BLOCK, width), jnp.float32),
            jax.ShapeDtypeStruct((BLOCK, width), jnp.bfloat16),
        ],
        scratch_shapes=[pltpu.VMEM((TILE, 8 * BLOCK), jnp.bfloat16)],
        compiler_params=params(24),
        cost_estimate=cost(2 * 8 * TILE * BLOCK * width, 11 * BLOCK * width * 2 + 8 * BLOCK * TILE * 2),
        name="apply_part",
    )(where, *mixing, *blocks)


def add(left, right):
    return (left.astype(jnp.float32) + right.astype(jnp.float32)).astype(jnp.bfloat16)


def gather_even(value, ring, pair, there=None):
    fore, back = send(value, ring + "_fore"), send(value, ring + "_back")
    there = send(value, pair) if there is None else there
    far = send(fore, ring + "_fore")
    there_fore = send(there, ring + "_fore")
    there_back = send(back, pair)
    there_far = send(there_fore, ring + "_fore")
    return [value, fore, back, far, there, there_fore, there_back, there_far]


def sum_over_col(tiles):
    chain = add(tiles[5], send(tiles[7], "z_back"))
    back = add(tiles[1], send(tiles[3], "z_back"))
    fore = add(tiles[2], send(tiles[6], "yl"))
    there = add(tiles[4], send(chain, "z_back"))
    total = tiles[0].astype(jnp.float32)
    total = total + send(back, "z_back").astype(jnp.float32)
    total = total + send(fore, "z_fore").astype(jnp.float32)
    total = total + send(there, "yl").astype(jnp.float32)
    return total.astype(jnp.bfloat16)


def on_device(iterate):
    total_cols = iterate.shape[1] * lax.axis_size("col")
    row, col = lax.axis_index("row"), lax.axis_index("col")
    where = jnp.stack([row >> 2, (row >> 1) & 1, row & 1, col >> 2, col & 3]).astype(jnp.int32)
    iterate, where = lax.optimization_barrier((iterate, where))

    half = BLOCK // 2
    across = send(iterate, "yh")
    other, back, low = lax.optimization_barrier(
        [send(iterate, "core"), send(iterate, "x_back"), send(iterate[half:], "x_fore")]
    )
    top = send(iterate[:half], "x_fore")
    far = [send(top, "x_fore"), send(low, "x_fore")]
    fore = jnp.concatenate([top, low], axis=0)
    near = gram_near(iterate, other, fore, back)
    far[0], near = lax.optimization_barrier((far[0], near))
    far = jnp.concatenate(far, axis=0)
    rows = (iterate, other, across, send(across, "core"))
    gram_left = sum_over_col(gram_tiles(where, *rows, fore, back, far, near))

    across_fore, across_back = send(across, "x_fore"), send(across, "x_back")
    gram_left, across_fore, across_back = lax.optimization_barrier((gram_left, across_fore, across_back))
    across_far = send(across_fore, "x_fore")
    gram = jnp.concatenate([gram_left[:BLOCK], send(gram_left[BLOCK:], "core")], axis=1)
    left, right = gather_even(gram_left, "z", "yh"), gather_even(gram, "x", "yl")
    mine, theirs = square_part(where, left, right)
    square = mine + send(theirs, "core").astype(jnp.float32)
    mixing = (cubic_coef * gram_left.astype(jnp.float32) + quintic_coef * square).astype(jnp.bfloat16)

    there = send(mixing, "turn_yl")
    pieces = gather_even(send(mixing, "turn"), "z", "yl", there)
    blocks = [iterate, fore, back, far, across, across_fore, across_back, across_far]
    depth = iterate.shape[1]
    update = []
    for begin in (0, depth // 2):
        mine, theirs = apply_part(begin, depth // 2, where, pieces, blocks)
        update.append(mine + send(theirs, "core").astype(jnp.float32))
    return (math.sqrt(total_cols) * jnp.concatenate(update, axis=1)).astype(jnp.bfloat16)


def solution(mesh):
    return jax.shard_map(
        on_device,
        mesh=mesh,
        in_specs=(P("row", "col"),),
        out_specs=P("row", "col"),
        check_vma=False,
    )
```

```python
import functools
import math

import jax
import jax.numpy as jnp
from jax import lax
from jax.experimental import pallas as pl
from jax.experimental.pallas import tpu as pltpu
from jax.sharding import PartitionSpec as P

linear_coef = 3.4445
cubic_coef = -4.775
quintic_coef = 2.0315

NX, NY, NC, NZ = 4, 2, 2, 4
BLOCK = 256
TILE = 2 * BLOCK
STRIP = 768
MIB = 1 << 20


def pairs(move):
    out = []
    for x in range(NX):
        for yh in range(NY):
            for core in range(NC):
                for yl in range(NY):
                    for z in range(NZ):
                        source = ((x * 2 + yh) * 2 + core) * 8 + yl * 4 + z
                        a, b, c, d, e = move(x, yh, core, yl, z)
                        a, e = a % NX, e % NZ
                        out.append((source, ((a * 2 + b) * 2 + c) * 8 + d * 4 + e))
    return out


def way(core):
    return 1 - 2 * core


MOVES = {
    "core": lambda x, yh, c, yl, z: (x, yh, 1 - c, yl, z),
    "yh": lambda x, yh, c, yl, z: (x, 1 - yh, c, yl, z),
    "yl": lambda x, yh, c, yl, z: (x, yh, c, 1 - yl, z),
    "turn": lambda x, yh, c, yl, z: (x, yl, c, yh, z),
    "turn_yl": lambda x, yh, c, yl, z: (x, yl, c, 1 - yh, z),
    "x_fore": lambda x, yh, c, yl, z: (x + way(c), yh, c, yl, z),
    "x_back": lambda x, yh, c, yl, z: (x - way(c), yh, c, yl, z),
    "z_fore": lambda x, yh, c, yl, z: (x, yh, c, yl, z + way(c)),
    "z_back": lambda x, yh, c, yl, z: (x, yh, c, yl, z - way(c)),
}


def send(value, move):
    return lax.ppermute(value, ("row", "col"), pairs(MOVES[move]))


def place(delta, core):
    delta = lax.rem(delta + 8, 4)
    side = jnp.where(delta == 3 - 2 * core, 1, 2)
    return jnp.where(delta == 0, 0, jnp.where(delta == 2, 3, side))


def ahead(position, core):
    return (0, 2 * core - 1, 1 - 2 * core, 2)[position]


def nt(left, right):
    return lax.dot_general(left, right, (((1,), (1,)), ((), ())), preferred_element_type=jnp.float32)


def nn(left, right):
    return lax.dot_general(left, right, (((1,), (0,)), ((), ())), preferred_element_type=jnp.float32)


def gram_near_kernel(own, other, fore, back, out):
    for r, rows in enumerate((own, other)):
        for q, cols in enumerate((own, fore, back)):
            part = nt(rows[...], cols[...])
            out[q, r * BLOCK : (r + 1) * BLOCK] = part.astype(out.dtype)


def gram_kernel(where, own, other, across, across_other, fore, back, far, near, *rest):
    outs, tiles = rest[:8], rest[8]
    x, yh, core, yl, z = (where[i] for i in range(5))
    tiles[0, :3] = near[...]
    for r, rows in enumerate((own, other)):
        part = nt(rows[...], far[...])
        tiles[0, 3, r * BLOCK : (r + 1) * BLOCK] = part.astype(tiles.dtype)
    for r, rows in enumerate((across, across_other)):
        for q, cols in enumerate((own, fore, back, far)):
            part = nt(rows[...], cols[...])
            tiles[1, q, r * BLOCK : (r + 1) * BLOCK] = part.astype(tiles.dtype)
    for index, out in enumerate(outs):
        row = lax.rem(yl + index // 4 + yh, 2)
        col = place(z + ahead(index % 4, core) - x, core)
        out[...] = tiles[row, col]


def square_kernel(others, where, *rest):
    left, right, (out, held) = rest[:8], rest[8:16], rest[16:]
    x, yh, core, yl, z = (where[i] for i in range(5))
    for index in range(8):
        row = lax.rem(yh + index // 4 + yl, 2)
        col = place(x + ahead(index % 4, core) - z, core)
        depth = pl.ds(pl.multiple_of((row * 4 + col) * BLOCK, BLOCK), BLOCK)
        held[depth] = right[index][:, others * BLOCK : (others + 1) * BLOCK]
    total = nn(jnp.concatenate([ref[...] for ref in left], axis=1), held[...]).astype(out.dtype)
    if others:
        out[:BLOCK], out[BLOCK:] = total[BLOCK:], total[:BLOCK]
    else:
        out[...] = total


def apply_kernel(begin, where, *rest):
    mixing, blocks, (mine, theirs, held) = rest[:8], rest[8:16], rest[16:]
    x, yh, core, yl, z = (where[i] for i in range(5))
    for index in range(8):
        row = lax.rem(yl + index // 4 + yh, 2)
        col = place(z + ahead(index % 4, core) - x, core)
        lanes = pl.ds(pl.multiple_of((row * 4 + col) * BLOCK, BLOCK), BLOCK)
        held[:, lanes] = mixing[index][...]

    for start in range(0, mine.shape[1], STRIP):
        columns = slice(begin + start, begin + start + STRIP)
        total = nn(held[...], jnp.concatenate([block[:, columns] for block in blocks], axis=0))
        theirs[:, start : start + STRIP] = total[BLOCK:].astype(theirs.dtype)
        total = total[:BLOCK] + linear_coef * blocks[0][:, columns].astype(jnp.float32)
        mine[:, start : start + STRIP] = total


def params(mib):
    return pltpu.CompilerParams(vmem_limit_bytes=mib * MIB)


def smem():
    return pl.BlockSpec(memory_space=pltpu.SMEM)


def whole():
    return pl.BlockSpec(memory_space=pltpu.VMEM)


def cost(flops, moved):
    return pl.CostEstimate(flops=flops, bytes_accessed=moved, transcendentals=0)


def gram_near(own, other, fore, back):
    depth = own.shape[1]
    return pl.pallas_call(
        gram_near_kernel,
        in_specs=[whole() for _ in range(4)],
        out_specs=whole(),
        out_shape=jax.ShapeDtypeStruct((3, TILE, BLOCK), jnp.bfloat16),
        compiler_params=params(24),
        cost_estimate=cost(2 * 3 * BLOCK * TILE * depth, 4 * BLOCK * depth * 2 + 3 * BLOCK * TILE * 2),
        name="gram_near",
    )(own, other, fore, back)


def gram_tiles(where, own, other, across, across_other, fore, back, far, near):
    depth = own.shape[1]
    return pl.pallas_call(
        gram_kernel,
        in_specs=[smem()] + [whole() for _ in range(8)],
        out_specs=[whole() for _ in range(8)],
        out_shape=[jax.ShapeDtypeStruct((TILE, BLOCK), jnp.bfloat16) for _ in range(8)],
        scratch_shapes=[pltpu.VMEM((2, 4, TILE, BLOCK), jnp.bfloat16)],
        compiler_params=params(24),
        cost_estimate=cost(2 * 5 * BLOCK * TILE * depth, 7 * BLOCK * depth * 2 + 11 * BLOCK * TILE * 2),
        name="gram_tiles",
    )(where, own, other, across, across_other, fore, back, far, near)


def square_part(others, where, left, right):
    return pl.pallas_call(
        functools.partial(square_kernel, others),
        in_specs=[smem()] + [whole() for _ in range(16)],
        out_specs=whole(),
        out_shape=jax.ShapeDtypeStruct((TILE, BLOCK), jnp.bfloat16 if others else jnp.float32),
        scratch_shapes=[pltpu.VMEM((8 * BLOCK, BLOCK), jnp.bfloat16)],
        compiler_params=params(24),
        cost_estimate=cost(2 * 8 * TILE * BLOCK * BLOCK, 13 * BLOCK * TILE * 2),
        name="square_theirs" if others else "square_part",
    )(where, *left, *right)


def apply_part(begin, width, where, mixing, blocks):
    return pl.pallas_call(
        functools.partial(apply_kernel, begin),
        in_specs=[smem()] + [whole() for _ in range(16)],
        out_specs=[whole(), whole()],
        out_shape=[
            jax.ShapeDtypeStruct((BLOCK, width), jnp.float32),
            jax.ShapeDtypeStruct((BLOCK, width), jnp.bfloat16),
        ],
        scratch_shapes=[pltpu.VMEM((TILE, 8 * BLOCK), jnp.bfloat16)],
        compiler_params=params(24),
        cost_estimate=cost(2 * 8 * TILE * BLOCK * width, 11 * BLOCK * width * 2 + 8 * BLOCK * TILE * 2),
        name="apply_part",
    )(where, *mixing, *blocks)


def add(left, right):
    return (left.astype(jnp.float32) + right.astype(jnp.float32)).astype(jnp.bfloat16)


def gather_even(value, ring, pair, there=None):
    fore, back = send(value, ring + "_fore"), send(value, ring + "_back")
    there = send(value, pair) if there is None else there
    far = send(fore, ring + "_fore")
    there_fore = send(there, ring + "_fore")
    there_back = send(back, pair)
    there_far = send(there_fore, ring + "_fore")
    return [value, fore, back, far, there, there_fore, there_back, there_far]


def sum_over_col(tiles):
    chain = add(tiles[5], send(tiles[7], "z_back"))
    back = add(tiles[1], send(tiles[3], "z_back"))
    fore = add(tiles[2], send(tiles[6], "yl"))
    there = add(tiles[4], send(chain, "z_back"))
    total = tiles[0].astype(jnp.float32)
    total = total + send(back, "z_back").astype(jnp.float32)
    total = total + send(fore, "z_fore").astype(jnp.float32)
    total = total + send(there, "yl").astype(jnp.float32)
    return total.astype(jnp.bfloat16)


def on_device(iterate):
    total_cols = iterate.shape[1] * lax.axis_size("col")
    row, col = lax.axis_index("row"), lax.axis_index("col")
    where = jnp.stack([row >> 2, (row >> 1) & 1, row & 1, col >> 2, col & 3]).astype(jnp.int32)
    iterate, where = lax.optimization_barrier((iterate, where))

    half = BLOCK // 2
    across = send(iterate, "yh")
    other, back, low = lax.optimization_barrier(
        [send(iterate, "core"), send(iterate, "x_back"), send(iterate[half:], "x_fore")]
    )
    top = send(iterate[:half], "x_fore")
    far = [send(top, "x_fore"), send(low, "x_fore")]
    fore = jnp.concatenate([top, low], axis=0)
    near = gram_near(iterate, other, fore, back)
    far[0], near = lax.optimization_barrier((far[0], near))
    far = jnp.concatenate(far, axis=0)
    rows = (iterate, other, across, send(across, "core"))
    gram_left = sum_over_col(gram_tiles(where, *rows, fore, back, far, near))

    across_fore, across_back = send(across, "x_fore"), send(across, "x_back")
    gram_left, across_fore, across_back = lax.optimization_barrier((gram_left, across_fore, across_back))
    across_far = send(across_fore, "x_fore")
    gram = jnp.concatenate([gram_left[:BLOCK], send(gram_left[BLOCK:], "core")], axis=1)
    left, right = gather_even(gram_left, "z", "yh"), gather_even(gram, "x", "yl")
    theirs = send(square_part(1, where, left, right), "core")
    square = square_part(0, where, left, right) + theirs.astype(jnp.float32)
    mixing = (cubic_coef * gram_left.astype(jnp.float32) + quintic_coef * square).astype(jnp.bfloat16)

    there = send(mixing, "turn_yl")
    pieces = gather_even(send(mixing, "turn"), "z", "yl", there)
    blocks = [iterate, fore, back, far, across, across_fore, across_back, across_far]
    depth = iterate.shape[1]
    update = []
    for begin in (0, depth // 2):
        mine, theirs = apply_part(begin, depth // 2, where, pieces, blocks)
        update.append(mine + send(theirs, "core").astype(jnp.float32))
    return (math.sqrt(total_cols) * jnp.concatenate(update, axis=1)).astype(jnp.bfloat16)


def solution(mesh):
    return jax.shard_map(
        on_device,
        mesh=mesh,
        in_specs=(P("row", "col"),),
        out_specs=P("row", "col"),
        check_vma=False,
    )
```

```python
import functools
import math

import jax
import jax.numpy as jnp
from jax import lax
from jax.experimental import pallas as pl
from jax.experimental.pallas import tpu as pltpu
from jax.sharding import PartitionSpec as P

linear_coef = 3.4445
cubic_coef = -4.775
quintic_coef = 2.0315

NX, NY, NC, NZ = 4, 2, 2, 4
BLOCK = 256
TILE = 2 * BLOCK
STRIP = 768
MIB = 1 << 20


def pairs(move):
    out = []
    for x in range(NX):
        for yh in range(NY):
            for core in range(NC):
                for yl in range(NY):
                    for z in range(NZ):
                        source = ((x * 2 + yh) * 2 + core) * 8 + yl * 4 + z
                        a, b, c, d, e = move(x, yh, core, yl, z)
                        a, e = a % NX, e % NZ
                        out.append((source, ((a * 2 + b) * 2 + c) * 8 + d * 4 + e))
    return out


def way(core):
    return 1 - 2 * core


MOVES = {
    "core": lambda x, yh, c, yl, z: (x, yh, 1 - c, yl, z),
    "yh": lambda x, yh, c, yl, z: (x, 1 - yh, c, yl, z),
    "yl": lambda x, yh, c, yl, z: (x, yh, c, 1 - yl, z),
    "turn": lambda x, yh, c, yl, z: (x, yl, c, yh, z),
    "turn_yl": lambda x, yh, c, yl, z: (x, yl, c, 1 - yh, z),
    "x_fore": lambda x, yh, c, yl, z: (x + way(c), yh, c, yl, z),
    "x_back": lambda x, yh, c, yl, z: (x - way(c), yh, c, yl, z),
    "z_fore": lambda x, yh, c, yl, z: (x, yh, c, yl, z + way(c)),
    "z_back": lambda x, yh, c, yl, z: (x, yh, c, yl, z - way(c)),
}


def send(value, move):
    return lax.ppermute(value, ("row", "col"), pairs(MOVES[move]))


def place(delta, core):
    delta = lax.rem(delta + 8, 4)
    side = jnp.where(delta == 3 - 2 * core, 1, 2)
    return jnp.where(delta == 0, 0, jnp.where(delta == 2, 3, side))


def ahead(position, core):
    return (0, 2 * core - 1, 1 - 2 * core, 2)[position]


def nt(left, right):
    return lax.dot_general(left, right, (((1,), (1,)), ((), ())), preferred_element_type=jnp.float32)


def nn(left, right):
    return lax.dot_general(left, right, (((1,), (0,)), ((), ())), preferred_element_type=jnp.float32)


def gram_near_kernel(first, second, own, fore, back, out):
    for r, rows in enumerate((first, second)):
        for q, cols in enumerate((own, fore, back)):
            part = nt(rows[...], cols[...])
            out[q, r * BLOCK : (r + 1) * BLOCK] = part.astype(out.dtype)


def gram_kernel(where, own, other, across, across_other, far, near, near_across, *rest):
    outs, tiles = rest[:8], rest[8]
    x, yh, core, yl, z = (where[i] for i in range(5))
    tiles[0, :3] = near[...]
    tiles[1, :3] = near_across[...]
    for r, rows in enumerate((own, other, across, across_other)):
        part = nt(rows[...], far[...])
        tiles[r // 2, 3, (r % 2) * BLOCK : (r % 2 + 1) * BLOCK] = part.astype(tiles.dtype)
    for index, out in enumerate(outs):
        row = lax.rem(yl + index // 4 + yh, 2)
        col = place(z + ahead(index % 4, core) - x, core)
        out[...] = tiles[row, col]


def square_kernel(others, where, *rest):
    left, right, (out, held) = rest[:8], rest[8:16], rest[16:]
    x, yh, core, yl, z = (where[i] for i in range(5))
    for index in range(8):
        row = lax.rem(yh + index // 4 + yl, 2)
        col = place(x + ahead(index % 4, core) - z, core)
        depth = pl.ds(pl.multiple_of((row * 4 + col) * BLOCK, BLOCK), BLOCK)
        held[depth] = right[index][:, others * BLOCK : (others + 1) * BLOCK]
    total = nn(jnp.concatenate([ref[...] for ref in left], axis=1), held[...]).astype(out.dtype)
    if others:
        out[:BLOCK], out[BLOCK:] = total[BLOCK:], total[:BLOCK]
    else:
        out[...] = total


def apply_kernel(begin, where, *rest):
    mixing, blocks, (mine, theirs, held) = rest[:8], rest[8:16], rest[16:]
    x, yh, core, yl, z = (where[i] for i in range(5))
    for index in range(8):
        row = lax.rem(yl + index // 4 + yh, 2)
        col = place(z + ahead(index % 4, core) - x, core)
        lanes = pl.ds(pl.multiple_of((row * 4 + col) * BLOCK, BLOCK), BLOCK)
        held[:, lanes] = mixing[index][...]

    for start in range(0, mine.shape[1], STRIP):
        columns = slice(begin + start, begin + start + STRIP)
        total = nn(held[...], jnp.concatenate([block[:, columns] for block in blocks], axis=0))
        theirs[:, start : start + STRIP] = total[BLOCK:].astype(theirs.dtype)
        total = total[:BLOCK] + linear_coef * blocks[0][:, columns].astype(jnp.float32)
        mine[:, start : start + STRIP] = total


def params(mib):
    return pltpu.CompilerParams(vmem_limit_bytes=mib * MIB)


def smem():
    return pl.BlockSpec(memory_space=pltpu.SMEM)


def whole():
    return pl.BlockSpec(memory_space=pltpu.VMEM)


def cost(flops, moved):
    return pl.CostEstimate(flops=flops, bytes_accessed=moved, transcendentals=0)


def gram_near(first, second, own, fore, back):
    depth = own.shape[1]
    return pl.pallas_call(
        gram_near_kernel,
        in_specs=[whole() for _ in range(5)],
        out_specs=whole(),
        out_shape=jax.ShapeDtypeStruct((3, TILE, BLOCK), jnp.bfloat16),
        compiler_params=params(24),
        cost_estimate=cost(2 * 3 * BLOCK * TILE * depth, 4 * BLOCK * depth * 2 + 3 * BLOCK * TILE * 2),
        name="gram_near",
    )(first, second, own, fore, back)


def gram_tiles(where, own, other, across, across_other, far, near, near_across):
    depth = own.shape[1]
    return pl.pallas_call(
        gram_kernel,
        in_specs=[smem()] + [whole() for _ in range(7)],
        out_specs=[whole() for _ in range(8)],
        out_shape=[jax.ShapeDtypeStruct((TILE, BLOCK), jnp.bfloat16) for _ in range(8)],
        scratch_shapes=[pltpu.VMEM((2, 4, TILE, BLOCK), jnp.bfloat16)],
        compiler_params=params(24),
        cost_estimate=cost(2 * 2 * BLOCK * TILE * depth, 5 * BLOCK * depth * 2 + 14 * BLOCK * TILE * 2),
        name="gram_tiles",
    )(where, own, other, across, across_other, far, near, near_across)


def square_part(others, where, left, right):
    return pl.pallas_call(
        functools.partial(square_kernel, others),
        in_specs=[smem()] + [whole() for _ in range(16)],
        out_specs=whole(),
        out_shape=jax.ShapeDtypeStruct((TILE, BLOCK), jnp.bfloat16 if others else jnp.float32),
        scratch_shapes=[pltpu.VMEM((8 * BLOCK, BLOCK), jnp.bfloat16)],
        compiler_params=params(24),
        cost_estimate=cost(2 * 8 * TILE * BLOCK * BLOCK, 13 * BLOCK * TILE * 2),
        name="square_theirs" if others else "square_part",
    )(where, *left, *right)


def apply_part(begin, width, where, mixing, blocks):
    return pl.pallas_call(
        functools.partial(apply_kernel, begin),
        in_specs=[smem()] + [whole() for _ in range(16)],
        out_specs=[whole(), whole()],
        out_shape=[
            jax.ShapeDtypeStruct((BLOCK, width), jnp.float32),
            jax.ShapeDtypeStruct((BLOCK, width), jnp.bfloat16),
        ],
        scratch_shapes=[pltpu.VMEM((TILE, 8 * BLOCK), jnp.bfloat16)],
        compiler_params=params(24),
        cost_estimate=cost(2 * 8 * TILE * BLOCK * width, 11 * BLOCK * width * 2 + 8 * BLOCK * TILE * 2),
        name="apply_part",
    )(where, *mixing, *blocks)


def add(left, right):
    return (left.astype(jnp.float32) + right.astype(jnp.float32)).astype(jnp.bfloat16)


def gather_even(value, ring, pair, there=None):
    fore, back = send(value, ring + "_fore"), send(value, ring + "_back")
    there = send(value, pair) if there is None else there
    far = send(fore, ring + "_fore")
    there_fore = send(there, ring + "_fore")
    there_back = send(back, pair)
    there_far = send(there_fore, ring + "_fore")
    return [value, fore, back, far, there, there_fore, there_back, there_far]


def sum_over_col(tiles):
    chain = add(tiles[5], send(tiles[7], "z_back"))
    back = add(tiles[1], send(tiles[3], "z_back"))
    fore = add(tiles[2], send(tiles[6], "yl"))
    there = add(tiles[4], send(chain, "z_back"))
    total = tiles[0].astype(jnp.float32)
    total = total + send(back, "z_back").astype(jnp.float32)
    total = total + send(fore, "z_fore").astype(jnp.float32)
    total = total + send(there, "yl").astype(jnp.float32)
    return total.astype(jnp.bfloat16)


def on_device(iterate):
    total_cols = iterate.shape[1] * lax.axis_size("col")
    row, col = lax.axis_index("row"), lax.axis_index("col")
    where = jnp.stack([row >> 2, (row >> 1) & 1, row & 1, col >> 2, col & 3]).astype(jnp.int32)
    iterate, where = lax.optimization_barrier((iterate, where))

    half = BLOCK // 2
    across = send(iterate, "yh")
    other, back, low = lax.optimization_barrier(
        [send(iterate, "core"), send(iterate, "x_back"), send(iterate[half:], "x_fore")]
    )
    top = send(iterate[:half], "x_fore")
    far = [send(top, "x_fore"), send(low, "x_fore")]
    fore = jnp.concatenate([top, low], axis=0)
    near = gram_near(iterate, other, iterate, fore, back)
    rows = (iterate, other, across, send(across, "core"))
    near_across = gram_near(rows[2], rows[3], iterate, fore, back)
    far[0], near, near_across = lax.optimization_barrier((far[0], near, near_across))
    far = jnp.concatenate(far, axis=0)
    gram_left = sum_over_col(gram_tiles(where, *rows, far, near, near_across))

    across_fore, across_back = send(across, "x_fore"), send(across, "x_back")
    gram_left, across_fore, across_back = lax.optimization_barrier((gram_left, across_fore, across_back))
    across_far = send(across_fore, "x_fore")
    gram = jnp.concatenate([gram_left[:BLOCK], send(gram_left[BLOCK:], "core")], axis=1)
    left, right = gather_even(gram_left, "z", "yh"), gather_even(gram, "x", "yl")
    theirs = send(square_part(1, where, left, right), "core")
    square = square_part(0, where, left, right) + theirs.astype(jnp.float32)
    mixing = (cubic_coef * gram_left.astype(jnp.float32) + quintic_coef * square).astype(jnp.bfloat16)

    there = send(mixing, "turn_yl")
    pieces = gather_even(send(mixing, "turn"), "z", "yl", there)
    blocks = [iterate, fore, back, far, across, across_fore, across_back, across_far]
    depth = iterate.shape[1]
    update = []
    for begin in (0, depth // 2):
        mine, theirs = apply_part(begin, depth // 2, where, pieces, blocks)
        update.append(mine + send(theirs, "core").astype(jnp.float32))
    return (math.sqrt(total_cols) * jnp.concatenate(update, axis=1)).astype(jnp.bfloat16)


def solution(mesh):
    return jax.shard_map(
        on_device,
        mesh=mesh,
        in_specs=(P("row", "col"),),
        out_specs=P("row", "col"),
        check_vma=False,
    )
```
